32 devices in a mesh: grp: 8 (over z, core), tm: 4 (over y, x).
Axes of the slice: x: 2, y: 2, z: 4, core: 2. Of those that a mesh axis runs over, the one named last changes fastest.
Arguments:
- features: bfloat16 [32, 1024, 1024], P('grp', 'tm'), may hold values from -40 to 40
- frame_counts: int32 [32], P('grp'), may hold values from 256 to 1024
- pool_query: bfloat16 [8, 1024], replicated, may hold values from -4 to 4
- w_proj: bfloat16 [1024, 512], replicated, may hold values from -0.1875 to 0.1875
- doc_embed: bfloat16 [512, 512], P(('grp', 'tm')), may hold values from -0.25 to 0.25
- doc_index: int32 [32], replicated, may hold values from 0 to 511
Outputs:
- loss: float32 [32], P('grp')
- speech_grad: float32 [32, 512], P('grp')
- doc_grad: float32 [512, 512], P(('grp', 'tm'))
The draws below stay inside these ranges and needn't reach their ends.
All inputs are finite; a program needn't handle non-finite values.
Results may differ from the reference program's by a relative error of at most 0.0044.
Values may be sent and summed in bfloat16 or wider, within the bound.
No kernel may reach another device: no remote copies, remote signals or barrier semaphores. Data moves between devices by JAX's collectives and lax.ppermute only.
A program may use at most 64 MiB of HBM per device.

```python
import math
import jax
import jax.numpy as jnp
from jax import lax

C = 1024
E = 512
H = 8
RECS = 32
FRAMES = 1024
DOCS = 512


def shared_query(key):
    return jnp.clip(jax.random.normal(jax.random.fold_in(key, 11), (H, C), jnp.float32), -4.0, 4.0)


def draw_pool_query(key, part):
    return shared_query(key).astype(jnp.bfloat16)


def draw_features(key, part):
    noise_key = jax.random.fold_in(key, 12)
    return jnp.clip(jax.random.normal(noise_key, (RECS, FRAMES, C), jnp.float32), -6.0, 6.0).astype(jnp.bfloat16)


def plant(drawn, key, least, top_value):
    shape = drawn.shape
    index_at = [jax.random.randint(jax.random.fold_in(key, axis), (), 0, shape[axis]) for axis in range(len(shape))]
    drawn = drawn.at[tuple(index_at)].set(least)
    longest = shape.index(max(shape))
    index_at[longest] = (index_at[longest] + 1) % shape[longest]
    return drawn.at[tuple(index_at)].set(top_value)


def steps_of(key, extent, shards, low, high):
    gain, own = 1.0, jax.random.fold_in(key, 6)
    for position, shards_of in shards:
        steps = jnp.exp(jax.random.uniform(jax.random.fold_in(own, position), (shards_of,), jnp.float32, low / len(shards), high / len(shards)))
        gain = gain * jnp.repeat(steps, extent[position] // shards_of).reshape([-1 if axis == position else 1 for axis in range(len(extent))])
    return gain


def scatter_about(stream_key, extent, deviation, reach, pieces=(), kind=jnp.bfloat16):
    values = deviation * jax.random.normal(stream_key, extent, jnp.float32)
    if pieces:
        values = values * steps_of(stream_key, extent, pieces, -0.22, 0.18)
    return jnp.clip(values, -reach, reach).astype(kind)


def setup_inputs(seed: int = 0) -> dict:
    seeds = jax.random.split(jax.random.key(seed), 7)
    return {
        "features": draw_features(jax.random.fold_in(seeds[6], 71), 0),
        "frame_counts": plant(jax.random.randint(seeds[1], (RECS,), FRAMES // 4, FRAMES + 1), jax.random.fold_in(seeds[1], 1), FRAMES // 4, FRAMES).astype(jnp.int32),
        "pool_query": draw_pool_query(jax.random.fold_in(seeds[6], 71), 0),
        "w_proj": scatter_about(seeds[3], (C, E), C ** -0.5, 0.1875),
        "doc_embed": scatter_about(seeds[4], (DOCS, E), E ** -0.5, 0.25, ((0, 32),)),
        "doc_index": plant(jax.random.randint(seeds[5], (RECS,), 0, DOCS), jax.random.fold_in(seeds[5], 1), 0, DOCS - 1).astype(jnp.int32),
    }


logit_scale = 10.0
logit_shift = -8.0
norm_eps = 1e-06

def reference(features, frame_counts, pool_query, w_proj, doc_embed, doc_index):

    def pool_one(inputs):
        frames, count = inputs
        values = jnp.dot(frames, w_proj, preferred_element_type=jnp.float32).astype(jnp.bfloat16)
        scores = jnp.dot(pool_query, frames.T, preferred_element_type=jnp.float32) / math.sqrt(C)
        valid = (jnp.arange(FRAMES, dtype=jnp.int32) < count)[None, :]
        masked = jnp.where(valid, scores, -1e+30)
        peak_score = lax.optimization_barrier(jnp.max(masked, axis=1))
        weights = jnp.where(valid, jnp.exp(masked - peak_score[:, None]), 0.0)
        totals = lax.optimization_barrier(jnp.sum(weights, axis=1))
        weights_b = weights.astype(jnp.bfloat16).astype(jnp.float32)
        head_values = values.astype(jnp.float32).reshape(FRAMES, H, E // H)
        numerator = jnp.einsum('hf,fhd->hd', weights_b, head_values)
        return (numerator / totals[:, None]).reshape(E)
    pooled = lax.map(pool_one, (features, frame_counts))
    speech = (pooled * lax.rsqrt(lax.optimization_barrier(jnp.sum(pooled * pooled, axis=1, keepdims=True)) + norm_eps)).astype(jnp.bfloat16)
    logits = logit_scale * jnp.dot(speech, doc_embed.T, preferred_element_type=jnp.float32) + logit_shift
    doc_ids = jnp.arange(DOCS, dtype=jnp.int32)
    labels = jnp.where(doc_index[:, None] == doc_ids[None, :], 1.0, -1.0)
    loss = lax.optimization_barrier(jnp.sum(jax.nn.softplus(-labels * logits), axis=1))
    grad_b = (-labels * jax.nn.sigmoid(-labels * logits)).astype(jnp.bfloat16)
    speech_grad = logit_scale * jnp.dot(grad_b, doc_embed, preferred_element_type=jnp.float32)
    doc_grad = logit_scale * jnp.dot(grad_b.T, speech, preferred_element_type=jnp.float32)
    return (loss, speech_grad, doc_grad)
```

```python
import math

import jax
import jax.numpy as jnp
from jax import lax
from jax.sharding import PartitionSpec as P

logit_scale = 10.0
logit_shift = -8.0
norm_eps = 1e-06
direct_limit = 8


def swap_pairs(count, stride, steps):
    return [(source, source ^ (steps * stride)) for source in range(count)]


def gathered(value, axis, stride, extent):
    count = lax.axis_size(axis)
    index = lax.axis_index(axis)
    place = (index // stride) % extent
    if extent <= direct_limit and extent & (extent - 1) == 0:
        parts = [value] + [
            lax.ppermute(value, axis, swap_pairs(count, stride, steps)) for steps in range(1, extent)
        ]
        places = [place ^ steps for steps in range(extent)]
        return parts, places
    groups = [
        [base + stride * step for step in range(extent)]
        for base in range(count)
        if (base // stride) % extent == 0
    ]
    whole = lax.all_gather(value, axis, axis_index_groups=groups)
    return [whole[step] for step in range(extent)], list(range(extent))


def split_two(value):
    high = value.astype(jnp.bfloat16)
    low = (value - high.astype(jnp.float32)).astype(jnp.bfloat16)
    return high, low


def pooled_part(features, frame_counts, pool_query, w_proj):
    rec_count, frame_dev, channels = features.shape
    heads = pool_query.shape[0]
    width = w_proj.shape[1]
    scores = jnp.einsum(
        "hc,rfc->rhf", pool_query, features, preferred_element_type=jnp.float32
    ) / math.sqrt(channels)
    positions = lax.axis_index("tm") * frame_dev + jnp.arange(frame_dev, dtype=jnp.int32)
    valid = (positions[None, :] < frame_counts[:, None])[:, None, :]
    masked = jnp.where(valid, scores, -1e30)
    peak = jnp.max(masked, axis=2).astype(jnp.bfloat16)
    weights = jnp.where(valid, jnp.exp(masked - peak.astype(jnp.float32)[:, :, None]), 0.0)
    totals = jnp.sum(weights, axis=2)
    high, low = split_two(weights)
    both = jnp.concatenate([high, low], axis=1)
    sums = jnp.einsum("rhf,rfc->rhc", both, features, preferred_element_type=jnp.float32)
    sums = (sums[:, :heads] + sums[:, heads:]).reshape(rec_count * heads, channels)
    high, low = split_two(sums)
    wide = jnp.dot(jnp.concatenate([high, low]), w_proj, preferred_element_type=jnp.float32)
    wide = (wide[: rec_count * heads] + wide[rec_count * heads :]).reshape(rec_count, heads, width)
    own = jnp.arange(width)[None, :] // (width // heads) == jnp.arange(heads)[:, None]
    numerator = jnp.sum(jnp.where(own[None], wide, 0.0), axis=1)
    return numerator, peak, totals


def pair_terms(speech, targets, docs, doc_ids):
    logits = (
        logit_scale * jnp.dot(speech, docs.T, preferred_element_type=jnp.float32) + logit_shift
    )
    labels = jnp.where(targets[:, None] == doc_ids[None, :], 1.0, -1.0)
    losses = jnp.sum(jax.nn.softplus(-labels * logits), axis=1)
    grad_b = (-labels * jax.nn.sigmoid(-labels * logits)).astype(jnp.bfloat16)
    return losses, grad_b


def body(features, frame_counts, pool_query, w_proj, doc_embed, doc_index):
    rec_count, frame_dev, channels = features.shape
    heads = pool_query.shape[0]
    width = w_proj.shape[1]
    doc_dev = doc_embed.shape[0]
    group = lax.axis_index("grp")
    column = lax.axis_index("tm")
    group_count = lax.axis_size("grp")
    column_count = lax.axis_size("tm")
    cores = 2 if group_count % 2 == 0 else 1
    layers = group_count // cores
    core = group % cores

    def doc_start(layer, core, column):
        return ((layer * cores + core) * column_count + column) * doc_dev

    doc_parts, doc_layers = gathered(doc_embed, "grp", cores, layers)
    numerator, peak, totals = pooled_part(features, frame_counts, pool_query, w_proj)

    high, low = split_two(numerator)
    total_high, total_low = split_two(totals)
    stats = jnp.concatenate([peak, total_high, total_low], axis=1)
    stats = jnp.pad(stats, ((0, 0), (0, width - 3 * heads)))
    payload = jnp.concatenate(doc_parts + [high, low, stats])
    doc_rows = layers * doc_dev
    parts, columns = gathered(payload, "tm", 1, column_count)

    stats = jnp.stack([part[doc_rows + 2 * rec_count :, : 3 * heads] for part in parts]).astype(jnp.float32)
    peaks = stats[:, :, :heads]
    top = jnp.max(peaks, axis=0)
    shares = jnp.exp(peaks - top[None])
    all_totals = jnp.sum(shares * (stats[:, :, heads : 2 * heads] + stats[:, :, 2 * heads :]), axis=0)
    scale = shares / all_totals[None]
    scale = jnp.repeat(scale, width // heads, axis=2)
    numerators = jnp.stack(
        [
            part[doc_rows : doc_rows + rec_count].astype(jnp.float32)
            + part[doc_rows + rec_count : doc_rows + 2 * rec_count].astype(jnp.float32)
            for part in parts
        ]
    )
    pooled = jnp.sum(numerators * scale, axis=0)
    speech = (
        pooled * lax.rsqrt(jnp.sum(pooled * pooled, axis=1, keepdims=True) + norm_eps)
    ).astype(jnp.bfloat16)

    speech_parts, layer_list = gathered(speech, "grp", cores, layers)
    docs = jnp.concatenate([part[:doc_rows] for part in parts])
    doc_ids = jnp.concatenate(
        [
            doc_start(layer, core, col) + jnp.arange(doc_dev, dtype=jnp.int32)
            for col in columns
            for layer in doc_layers
        ]
    )
    own_targets = lax.dynamic_slice_in_dim(doc_index, group * rec_count, rec_count)
    loss, grad_b = pair_terms(speech, own_targets, docs, doc_ids)
    speech_grad = jnp.dot(grad_b, docs, preferred_element_type=jnp.float32)
    rows = jnp.concatenate(speech_parts)
    rec_ids = jnp.concatenate(
        [
            (layer * cores + core) * rec_count + jnp.arange(rec_count, dtype=jnp.int32)
            for layer in layer_list
        ]
    )
    if cores == 2:
        pairs = swap_pairs(group_count, 1, 1)
        other_docs = lax.ppermute(docs, "grp", pairs)
        other_rows = lax.ppermute(rows, "grp", pairs)
        shift = (1 - 2 * core) * column_count * doc_dev
        other_loss, other_grad = pair_terms(speech, own_targets, other_docs, doc_ids + shift)
        loss = loss + other_loss
        speech_grad = speech_grad + jnp.dot(other_grad, other_docs, preferred_element_type=jnp.float32)
        rows = jnp.concatenate([rows, other_rows])
        rec_ids = jnp.concatenate([rec_ids, rec_ids + (1 - 2 * core) * rec_count])
    speech_grad = logit_scale * speech_grad

    rec_total = group_count * rec_count
    picks = rec_ids[:, None] == jnp.arange(rec_total, dtype=jnp.int32)[None, :]
    targets = jnp.sum(jnp.where(picks, doc_index[None, :], 0), axis=1)
    own_ids = (group * column_count + column) * doc_dev + jnp.arange(doc_dev, dtype=jnp.int32)
    _, grad_b = pair_terms(rows, targets, doc_embed, own_ids)
    doc_grad = logit_scale * jnp.dot(grad_b.T, rows, preferred_element_type=jnp.float32)
    return (loss, speech_grad, doc_grad)


def solution(mesh):
    placed = (P("grp", "tm", None), P("grp"), P(), P(), P(("grp", "tm"), None), P())
    return jax.shard_map(
        body,
        mesh=mesh,
        in_specs=placed,
        out_specs=(P("grp"), P("grp", None), P(("grp", "tm"), None)),
        check_vma=False,
    )
```

```python
import math

import jax
import jax.numpy as jnp
from jax import lax
from jax.experimental import pallas as pl
from jax.experimental.pallas import tpu as pltpu
from jax.sharding import PartitionSpec as P

logit_scale = 10.0
logit_shift = -8.0
norm_eps = 1e-06
direct_limit = 8
bf16 = jnp.bfloat16
f32 = jnp.float32
BY_ROWS = (((1,), (1,)), ((), ()))
VMEM = pl.BlockSpec(memory_space=pltpu.VMEM)


def in_vmem(kernel, outs, limit_mib, name):
    def call(*operands):
        return pl.pallas_call(
            kernel,
            out_shape=outs,
            in_specs=[VMEM] * len(operands),
            out_specs=jax.tree.map(lambda _: VMEM, outs),
            compiler_params=pltpu.CompilerParams(vmem_limit_bytes=limit_mib * 2**20),
            name=name,
        )(*operands)

    return call


def two_terms(value):
    high = value.astype(bf16)
    return high, (value - high.astype(f32)).astype(bf16)


def pool_kernel(
    scheme,
    blocks,
    counts_hbm,
    index_hbm,
    query_hbm,
    features_hbm,
    proj_hbm,
    out_ref,
    place_ref,
    at_ref,
    counts_ref,
    index_ref,
    query_ref,
    features_ref,
    proj_ref,
    sems,
):
    recs, frames, channels = features_ref.shape
    heads = query_ref.shape[0]
    width = proj_ref.shape[1]
    rows = recs * heads
    copies = [
        pltpu.make_async_copy(source, target, sems.at[n])
        for n, (source, target) in enumerate(
            [(counts_hbm, counts_ref), (query_hbm, query_ref)]
            + [(features_hbm.at[r], features_ref.at[r]) for r in range(recs)]
            + [(proj_hbm, proj_ref), (index_hbm, index_ref)]
        )
    ]
    for copy in copies:
        copy.start()
    copies[0].wait()
    copies[1].wait()
    query = query_ref[...]
    scores, limits = [], []
    start = lax.axis_index("tm") * frames
    for r in range(recs):
        copies[2 + r].wait()
        scores.append(lax.dot_general(query, features_ref[r], BY_ROWS, preferred_element_type=f32))
        limits.append(jnp.full((heads, 1), counts_ref[r] - start, jnp.int32))
    scores = jnp.concatenate(scores, 0) / math.sqrt(channels)
    valid = lax.broadcasted_iota(jnp.int32, (rows, frames), 1) < jnp.concatenate(limits, 0)
    masked = jnp.where(valid, scores, -1e30)
    peak = jnp.max(masked, axis=1, keepdims=True).astype(bf16).astype(f32)
    weights = jnp.where(valid, jnp.exp(masked - peak), 0.0)
    totals = jnp.sum(weights, axis=1, keepdims=True)
    high, low = two_terms(weights)
    sums = []
    for r in range(recs):
        part = slice(r * heads, (r + 1) * heads)
        both = jnp.concatenate([high[part], low[part]], 0)
        both = jnp.dot(both, features_ref[r], preferred_element_type=f32)
        sums.append(both[:heads] + both[heads:])
    high, low = two_terms(jnp.concatenate(sums, 0))
    copies[2 + recs].wait()
    wide = jnp.dot(jnp.concatenate([high, low], 0), proj_ref[...], preferred_element_type=f32)
    wide = wide[:rows] + wide[rows:]
    own = lax.broadcasted_iota(jnp.int32, (rows, width), 1) // (width // heads)
    own = own == lax.broadcasted_iota(jnp.int32, (rows, width), 0) % heads
    lane = lax.broadcasted_iota(jnp.int32, (rows, 128), 1)
    lane = lane == lax.broadcasted_iota(jnp.int32, (rows, 128), 0) % heads

    def over_heads(value):
        return jnp.concatenate(
            [jnp.sum(value[r * heads : (r + 1) * heads], 0, keepdims=True) for r in range(recs)], 0
        )

    pooled = over_heads(jnp.where(own, wide, 0.0))
    pooled_high = pooled.astype(bf16).astype(f32)
    totals = over_heads(jnp.where(lane, totals, 0.0))
    totals_high = totals.astype(bf16).astype(f32)
    peaks = over_heads(jnp.where(lane, peak, 0.0))
    stats = [peaks, totals_high, totals - totals_high, jnp.zeros((recs, width - 384), f32)]
    out_ref[...] = jnp.concatenate(
        [pooled_high, pooled - pooled_high, jnp.concatenate(stats, 1), jnp.zeros((recs, width), f32)], 0
    ).astype(bf16)

    copies[3 + recs].wait()
    group, column, tm = lax.axis_index("grp"), lax.axis_index("tm"), lax.axis_size("tm")
    layer, core = group // 2, group % 2
    docs_dev, far, by_column, by_far = scheme
    row = lax.broadcasted_iota(jnp.int32, place_ref.shape, 0)
    spot = lax.broadcasted_iota(jnp.int32, place_ref.shape, 1)
    place = jnp.full(place_ref.shape, -1, jnp.int32)
    for r in range(2 * recs):
        target = index_ref[(group ^ (r // recs)) * recs + r % recs]
        of_group, rest = target // (tm * docs_dev), target % (tm * docs_dev)
        of_layer = of_group // 2
        chunk = (of_layer ^ layer) % 2 + 2 * ((of_group ^ core) % 2)
        at = ((rest // docs_dev) ^ (column if by_column else 0)) * far
        at = (at + ((of_layer // 2) ^ (layer // 2 if by_far else 0))) * docs_dev + rest % docs_dev
        place = jnp.where((row == r) & (spot == chunk), at, place)
    place_ref[...] = place
    spot = lax.broadcasted_iota(jnp.int32, at_ref.shape, 1)
    ats = jnp.full(at_ref.shape, -1, jnp.int32)
    first = (group * tm + column) * docs_dev
    for n, block in enumerate(blocks):
        if block is not None:
            base = ((layer ^ block[0]) * 2 + (core ^ block[1])) * recs
            for r in range(recs):
                ats = jnp.where(spot == n * recs + r, index_ref[base + r] - first, ats)
    at_ref[...] = ats


def meet_kernel(recs, heads, *refs):
    parts, (send_ref, speech_ref) = refs[:-2], refs[-2:]
    doc_rows = parts[0].shape[0] - 4 * recs
    width = parts[0].shape[1]
    pools = [part[doc_rows:, :].astype(f32) for part in parts]
    peaks = [pool[2 * recs : 3 * recs, :128] for pool in pools]
    totals = [pool[2 * recs : 3 * recs, 128:256] + pool[2 * recs : 3 * recs, 256:384] for pool in pools]
    top = peaks[0]
    for peak in peaks[1:]:
        top = jnp.maximum(top, peak)
    shares = [jnp.exp(peak - top) for peak in peaks]
    whole = shares[0] * totals[0]
    for share, total in zip(shares[1:], totals[1:]):
        whole = whole + share * total
    used = lax.broadcasted_iota(jnp.int32, whole.shape, 1) < heads
    inverse = jnp.where(used, 1.0 / jnp.where(used, whole, 1.0), 0.0)
    high, low = two_terms(jnp.concatenate([share * inverse for share in shares], 0))
    spread = lax.broadcasted_iota(jnp.int32, (128, width), 1) // (width // heads)
    spread = (spread == lax.broadcasted_iota(jnp.int32, (128, width), 0)).astype(f32).astype(bf16)
    scales = jnp.dot(high, spread, preferred_element_type=f32) + jnp.dot(
        low, spread, preferred_element_type=f32
    )
    pooled = jnp.zeros((recs, width), f32)
    for n, pool in enumerate(pools):
        pooled = pooled + (pool[:recs] + pool[recs : 2 * recs]) * scales[n * recs : (n + 1) * recs]
    speech = pooled * lax.rsqrt(jnp.sum(pooled * pooled, axis=1, keepdims=True) + norm_eps)
    speech_ref[...] = speech.astype(bf16)
    for n, part in enumerate(parts):
        send_ref[n * doc_rows : (n + 1) * doc_rows, :] = part[:doc_rows, :]
    send_ref[len(parts) * doc_rows :, :] = jnp.concatenate(
        [speech, jnp.zeros((3 * recs, width), f32)], 0
    ).astype(bf16)


def pair_terms(logits, positive):
    logits = logit_scale * logits + logit_shift
    signed = jnp.where(positive, -logits, logits)
    losses = jnp.maximum(signed, 0.0) + jnp.log1p(jnp.exp(-jnp.abs(signed)))
    slopes = jax.nn.sigmoid(signed)
    return losses, jnp.where(positive, -slopes, slopes).astype(bf16)


def speech_terms(place_ref, chunk, speech, docs):
    logits = lax.dot_general(speech, docs, BY_ROWS, preferred_element_type=f32)
    positive = lax.broadcasted_iota(jnp.int32, logits.shape, 1) == place_ref[:, chunk : chunk + 1]
    losses, grad_b = pair_terms(logits, positive)
    grad = logit_scale * jnp.dot(grad_b, docs, preferred_element_type=f32)
    return jnp.sum(losses, axis=1, keepdims=True), grad


def own_kernel(recs, place_ref, own_ref, other_ref, both_ref, loss_ref, grad_ref):
    doc_rows = own_ref.shape[0] - 4 * recs
    mine = own_ref[doc_rows:, :].astype(f32)[:recs]
    other = other_ref[...].astype(f32)
    both = jnp.concatenate([mine, other, jnp.zeros((2 * recs, mine.shape[1]), f32)], 0).astype(bf16)
    loss, grad = speech_terms(place_ref, 0, both, own_ref[:doc_rows, :])
    both_ref[...] = both
    loss_ref[...] = jnp.broadcast_to(loss, loss_ref.shape)
    grad_ref[...] = grad


def near_kernel(recs, place_ref, both_ref, near_ref, loss_ref, grad_ref, loss_out, grad_out, send_ref):
    doc_rows = near_ref.shape[0] - 4 * recs
    loss, grad = speech_terms(place_ref, 1, both_ref[...], near_ref[:doc_rows, :])
    loss, grad = loss_ref[...] + loss, grad_ref[...] + grad
    loss_out[...] = loss[:recs]
    grad_out[...] = grad[:recs]
    loss, grad = loss[recs : 2 * recs], grad[recs : 2 * recs]
    grad_high = grad.astype(bf16).astype(f32)
    loss_high = loss.astype(bf16).astype(f32)
    loss_low = (loss - loss_high).astype(bf16).astype(f32)
    terms = [loss_high, loss_low, loss - loss_high - loss_low]
    terms.append(jnp.zeros((recs, grad.shape[1] - 384), f32))
    send_ref[...] = jnp.concatenate(
        [grad_high, grad - grad_high, jnp.concatenate(terms, 1), jnp.zeros_like(grad)], 0
    ).astype(bf16)


def last_kernel(recs, at_ref, docs_ref, loss_ref, grad_ref, came_ref, *refs):
    row_refs, (loss_out, speech_out, doc_out) = refs[:-3], refs[-3:]
    came = came_ref[came_ref.shape[0] - 4 * recs :, :].astype(f32)
    speech_out[...] = grad_ref[...] + came[:recs] + came[recs : 2 * recs]
    terms = came[2 * recs : 3 * recs]
    loss = loss_ref[...] + (terms[:, :128] + terms[:, 128:256] + terms[:, 256:384])
    diagonal = lax.broadcasted_iota(jnp.int32, (recs, 128), 0)
    diagonal = diagonal == lax.broadcasted_iota(jnp.int32, (recs, 128), 1)
    loss_out[...] = jnp.sum(jnp.where(diagonal, loss, 0.0), axis=0, keepdims=True)[:, :recs]
    if len(row_refs) == 1:
        rows = row_refs[0][...]
    else:
        rows = jnp.concatenate([ref[: 4 * recs, :] for ref in row_refs], 0)
    logits = lax.dot_general(docs_ref[...], rows, BY_ROWS, preferred_element_type=f32)
    positive = lax.broadcasted_iota(jnp.int32, logits.shape, 0) == at_ref[:1, : logits.shape[1]]
    _, grad_b = pair_terms(logits, positive)
    doc_out[...] = logit_scale * jnp.dot(grad_b, rows, preferred_element_type=f32)


def swap_pairs(count, stride, steps):
    return [(source, source ^ (steps * stride)) for source in range(count)]


def is_direct(extent):
    return extent <= direct_limit and extent & (extent - 1) == 0


def gathered(value, axis, stride, extent):
    count = lax.axis_size(axis)
    if is_direct(extent):
        parts = [value] + [
            lax.ppermute(value, axis, swap_pairs(count, stride, steps)) for steps in range(1, extent)
        ]
        return parts, True
    groups = [
        [base + stride * step for step in range(extent)]
        for base in range(count)
        if (base // stride) % extent == 0
    ]
    whole = lax.all_gather(value, axis, axis_index_groups=groups)
    return [whole[step] for step in range(extent)], False


def body(features, frame_counts, pool_query, w_proj, doc_embed, doc_index):
    recs, frames, channels = features.shape
    heads, width = pool_query.shape[0], w_proj.shape[1]
    docs_dev = doc_embed.shape[0]
    groups, columns = lax.axis_size("grp"), lax.axis_size("tm")
    layers = groups // 2
    direct = layers == 4

    far_docs, far_origin = gathered(doc_embed, "grp", 4, layers // 2)
    blocks = []
    if direct:
        blocks = [(0, 0), (0, 1), None, None, (1, 0), (2, 0), (3, 0), None, (1, 1), (2, 1), (3, 1)]
    scheme = (docs_dev, layers // 2, is_direct(columns), far_origin)
    pools, place, at = pl.pallas_call(
        lambda *refs: pool_kernel(scheme, blocks, *refs),
        out_shape=(
            jax.ShapeDtypeStruct((4 * recs, width), bf16),
            jax.ShapeDtypeStruct((4 * recs, 128), jnp.int32),
            jax.ShapeDtypeStruct((8, 128), jnp.int32),
        ),
        in_specs=[pl.BlockSpec(memory_space=pltpu.HBM)] * 5,
        out_specs=(VMEM, VMEM, VMEM),
        scratch_shapes=[
            pltpu.SMEM(frame_counts.shape, jnp.int32),
            pltpu.SMEM(doc_index.shape, jnp.int32),
            pltpu.VMEM(pool_query.shape, bf16),
            pltpu.VMEM(features.shape, bf16),
            pltpu.VMEM(w_proj.shape, bf16),
            pltpu.SemaphoreType.DMA((recs + 4,)),
        ],
        compiler_params=pltpu.CompilerParams(vmem_limit_bytes=12 * 2**20),
        name="pool",
    )(
        *[
            pltpu.with_memory_space_constraint(operand, pltpu.HBM)
            for operand in (frame_counts, doc_index, pool_query, features, w_proj)
        ]
    )
    parts, _ = gathered(jnp.concatenate(far_docs + [pools]), "tm", 1, columns)
    doc_rows = columns * (layers // 2) * docs_dev
    own, speech = in_vmem(
        lambda *refs: meet_kernel(recs, heads, *refs),
        (
            jax.ShapeDtypeStruct((doc_rows + 4 * recs, width), bf16),
            jax.ShapeDtypeStruct((recs, width), bf16),
        ),
        8,
        "meet",
    )(*parts)

    pairs = swap_pairs(groups, 1, 1)
    near = lax.ppermute(own, "grp", swap_pairs(groups, 2, 1))
    other = lax.ppermute(speech, "grp", pairs)
    mib = 8 + doc_rows // 128
    both, loss, grad = in_vmem(
        lambda *refs: own_kernel(recs, *refs),
        (
            jax.ShapeDtypeStruct((4 * recs, width), bf16),
            jax.ShapeDtypeStruct((4 * recs, 128), f32),
            jax.ShapeDtypeStruct((4 * recs, width), f32),
        ),
        mib,
        "own_docs",
    )(place, own, other)
    loss, grad, send = in_vmem(
        lambda *refs: near_kernel(recs, *refs),
        (
            jax.ShapeDtypeStruct((recs, 128), f32),
            jax.ShapeDtypeStruct((recs, width), f32),
            jax.ShapeDtypeStruct((4 * recs, width), bf16),
        ),
        mib,
        "near_docs",
    )(place, both, near, loss, grad)

    if direct:
        beyond = [lax.ppermute(speech, "grp", swap_pairs(groups, 2, steps)) for steps in (2, 3)]
        spare = jnp.zeros((recs, width), bf16)
        send = jnp.concatenate([near[doc_rows : doc_rows + recs], *beyond, spare, send])
    came = lax.ppermute(send, "grp", pairs)
    if direct:
        rows = (both, send, came)
    else:
        rows = (lax.all_gather(speech, "grp", tiled=True),)
        at = (doc_index - (lax.axis_index("grp") * columns + lax.axis_index("tm")) * docs_dev)[None, :]
    loss, speech_grad, doc_grad = in_vmem(
        lambda *refs: last_kernel(recs, *refs),
        (
            jax.ShapeDtypeStruct((1, recs), f32),
            jax.ShapeDtypeStruct((recs, width), f32),
            jax.ShapeDtypeStruct((docs_dev, width), f32),
        ),
        8,
        "last",
    )(at, doc_embed, loss, grad, came, *rows)
    return (loss[0], speech_grad, doc_grad)


def solution(mesh):
    placed = (P("grp", "tm", None), P("grp"), P(), P(), P(("grp", "tm"), None), P())
    return jax.shard_map(
        body,
        mesh=mesh,
        in_specs=placed,
        out_specs=(P("grp"), P("grp", None), P(("grp", "tm"), None)),
        check_vma=False,
    )
```

```python
import math

import jax
import jax.numpy as jnp
from jax import lax
from jax.experimental import pallas as pl
from jax.experimental.pallas import tpu as pltpu
from jax.sharding import PartitionSpec as P

logit_scale = 10.0
logit_shift = -8.0
norm_eps = 1e-06
direct_limit = 8
bf16 = jnp.bfloat16
f32 = jnp.float32
BY_ROWS = (((1,), (1,)), ((), ()))
VMEM = pl.BlockSpec(memory_space=pltpu.VMEM)


def in_vmem(kernel, outs, limit_mib, name):
    def call(*operands):
        return pl.pallas_call(
            kernel,
            out_shape=outs,
            in_specs=[VMEM] * len(operands),
            out_specs=jax.tree.map(lambda _: VMEM, outs),
            compiler_params=pltpu.CompilerParams(vmem_limit_bytes=limit_mib * 2**20),
            name=name,
        )(*operands)

    return call


def two_terms(value):
    high = value.astype(bf16)
    return high, (value - high.astype(f32)).astype(bf16)


def pool_kernel(
    scheme,
    blocks,
    counts_hbm,
    index_hbm,
    query_hbm,
    features_hbm,
    proj_hbm,
    docs_hbm,
    out_ref,
    place_ref,
    at_ref,
    counts_ref,
    index_ref,
    query_ref,
    features_ref,
    proj_ref,
    sems,
):
    recs, frames, channels = features_ref.shape
    heads = query_ref.shape[0]
    width = proj_ref.shape[1]
    rows = recs * heads
    docs_dev, by_column, by_layer = scheme
    copies = [
        pltpu.make_async_copy(source, target, sems.at[n])
        for n, (source, target) in enumerate(
            [(counts_hbm, counts_ref), (index_hbm, index_ref), (query_hbm, query_ref)]
            + [(features_hbm.at[r], features_ref.at[r]) for r in range(recs)]
            + [(proj_hbm, proj_ref), (docs_hbm, out_ref.at[:docs_dev])]
        )
    ]
    for copy in copies:
        copy.start()
    copies[1].wait()
    group, column, tm = lax.axis_index("grp"), lax.axis_index("tm"), lax.axis_size("tm")
    layer, core = group // 2, group % 2
    row = lax.broadcasted_iota(jnp.int32, place_ref.shape, 0)
    spot = lax.broadcasted_iota(jnp.int32, place_ref.shape, 1)
    place = jnp.full(place_ref.shape, -1, jnp.int32)
    for r in range(2 * recs):
        target = index_ref[(group ^ (r // recs)) * recs + r % recs]
        of_group, rest = target // (tm * docs_dev), target % (tm * docs_dev)
        of_layer = of_group // 2
        at = ((rest // docs_dev) ^ (column if by_column else 0)) * docs_dev + rest % docs_dev
        chunk = of_layer ^ layer if by_layer else 0
        at = at if by_layer else of_layer * tm * docs_dev + at
        chunk = jnp.where((of_group ^ core) % 2 == 0, chunk, -1)
        place = jnp.where((row == r) & (spot == chunk), at, place)
    place_ref[...] = place
    spot = lax.broadcasted_iota(jnp.int32, at_ref.shape, 1)
    ats = jnp.full(at_ref.shape, -1, jnp.int32)
    first = (group * tm + column) * docs_dev
    for n, block in enumerate(blocks):
        if block is not None:
            base = ((layer ^ block[0]) * 2 + (core ^ block[1])) * recs
            for r in range(recs):
                ats = jnp.where(spot == n * recs + r, index_ref[base + r] - first, ats)
    at_ref[...] = ats
    copies[0].wait()
    copies[2].wait()
    query = jnp.concatenate([query_ref[...].astype(f32), jnp.zeros((128 - heads, channels), f32)], 0).T.astype(bf16)
    start = lax.axis_index("tm") * frames
    spots = lax.broadcasted_iota(jnp.int32, (heads, frames), 1)
    scores, weights, peaks, totals, highs, lows = [], [], [], [], [], []
    for step in range(recs + 2):
        if step < recs:
            copies[3 + step].wait()
            scores.append(
                jnp.dot(features_ref[step], query, preferred_element_type=f32).T[:heads]
            )
        if 0 <= step - 1 < recs:
            r = step - 1
            valid = spots < counts_ref[r] - start
            masked = jnp.where(valid, scores[r] / math.sqrt(channels), -1e30)
            peak = jnp.max(masked, axis=1, keepdims=True).astype(bf16).astype(f32)
            weight = jnp.where(valid, jnp.exp(masked - peak), 0.0)
            peaks.append(peak)
            totals.append(jnp.sum(weight, axis=1, keepdims=True))
            weights.append(jnp.concatenate(two_terms(weight), 0))
        if 0 <= step - 2 < recs:
            r = step - 2
            both = jnp.dot(weights[r], features_ref[r], preferred_element_type=f32)
            high, low = two_terms(both[:heads] + both[heads:])
            highs.append(high)
            lows.append(low)
    peak, totals = jnp.concatenate(peaks, 0), jnp.concatenate(totals, 0)
    copies[3 + recs].wait()
    wide = jnp.dot(jnp.concatenate(highs + lows, 0), proj_ref[...], preferred_element_type=f32)
    wide = wide[:rows] + wide[rows:]
    own = lax.broadcasted_iota(jnp.int32, (rows, width), 1) // (width // heads)
    own = own == lax.broadcasted_iota(jnp.int32, (rows, width), 0) % heads
    lane = lax.broadcasted_iota(jnp.int32, (rows, 128), 1)
    lane = lane == lax.broadcasted_iota(jnp.int32, (rows, 128), 0) % heads

    def over_heads(value):
        return jnp.concatenate(
            [jnp.sum(value[r * heads : (r + 1) * heads], 0, keepdims=True) for r in range(recs)], 0
        )

    pooled = over_heads(jnp.where(own, wide, 0.0))
    pooled_high = pooled.astype(bf16).astype(f32)
    totals = over_heads(jnp.where(lane, totals, 0.0))
    totals_high = totals.astype(bf16).astype(f32)
    peaks = over_heads(jnp.where(lane, peak, 0.0))
    stats = [peaks, totals_high, totals - totals_high, jnp.zeros((recs, width - 384), f32)]
    copies[4 + recs].wait()
    out_ref[docs_dev:, :] = jnp.concatenate(
        [pooled_high, pooled - pooled_high, jnp.concatenate(stats, 1), jnp.zeros((recs, width), f32)], 0
    ).astype(bf16)


def meet_kernel(recs, heads, *refs):
    parts, (send_ref, speech_ref) = refs[:-2], refs[-2:]
    doc_rows = parts[0].shape[0] - 4 * recs
    width = parts[0].shape[1]
    pools = [part[doc_rows:, :].astype(f32) for part in parts]
    peaks = [pool[2 * recs : 3 * recs, :128] for pool in pools]
    totals = [pool[2 * recs : 3 * recs, 128:256] + pool[2 * recs : 3 * recs, 256:384] for pool in pools]
    top = peaks[0]
    for peak in peaks[1:]:
        top = jnp.maximum(top, peak)
    shares = [jnp.exp(peak - top) for peak in peaks]
    whole = shares[0] * totals[0]
    for share, total in zip(shares[1:], totals[1:]):
        whole = whole + share * total
    used = lax.broadcasted_iota(jnp.int32, whole.shape, 1) < heads
    inverse = jnp.where(used, 1.0 / jnp.where(used, whole, 1.0), 0.0)
    high, low = two_terms(jnp.concatenate([share * inverse for share in shares], 0))
    spread = lax.broadcasted_iota(jnp.int32, (128, width), 1) // (width // heads)
    spread = (spread == lax.broadcasted_iota(jnp.int32, (128, width), 0)).astype(f32).astype(bf16)
    scales = jnp.dot(high, spread, preferred_element_type=f32) + jnp.dot(
        low, spread, preferred_element_type=f32
    )
    pooled = jnp.zeros((recs, width), f32)
    for n, pool in enumerate(pools):
        pooled = pooled + (pool[:recs] + pool[recs : 2 * recs]) * scales[n * recs : (n + 1) * recs]
    speech = pooled * lax.rsqrt(jnp.sum(pooled * pooled, axis=1, keepdims=True) + norm_eps)
    speech_ref[...] = speech.astype(bf16)
    for n, part in enumerate(parts):
        send_ref[n * doc_rows : (n + 1) * doc_rows, :] = part[:doc_rows, :]
    send_ref[len(parts) * doc_rows :, :] = jnp.concatenate(
        [speech, jnp.zeros((recs, width), f32)], 0
    ).astype(bf16)


def pair_terms(logits, positive):
    logits = logit_scale * logits + logit_shift
    signed = jnp.where(positive, -logits, logits)
    losses = jnp.maximum(signed, 0.0) + jnp.log1p(jnp.exp(-jnp.abs(signed)))
    slopes = jax.nn.sigmoid(signed)
    return losses, jnp.where(positive, -slopes, slopes).astype(bf16)


def speech_terms(place_ref, chunk, speech, docs):
    logits = lax.dot_general(speech, docs, BY_ROWS, preferred_element_type=f32)
    positive = lax.broadcasted_iota(jnp.int32, logits.shape, 1) == place_ref[:, chunk : chunk + 1]
    losses, grad_b = pair_terms(logits, positive)
    grad = logit_scale * jnp.dot(grad_b, docs, preferred_element_type=f32)
    return jnp.sum(losses, axis=1, keepdims=True), grad


def first_docs_kernel(recs, place_ref, own_ref, other_ref, docs_ref, both_ref, loss_ref, grad_ref):
    mine = own_ref[own_ref.shape[0] - 2 * recs :, :].astype(f32)[:recs]
    other = other_ref[...].astype(f32)
    both = jnp.concatenate([mine, other, jnp.zeros((2 * recs, mine.shape[1]), f32)], 0).astype(bf16)
    loss, grad = speech_terms(place_ref, 0, both, docs_ref[: docs_ref.shape[0] - 2 * recs, :])
    both_ref[...] = both
    loss_ref[...] = jnp.broadcast_to(loss, loss_ref.shape)
    grad_ref[...] = grad


def next_docs_kernel(recs, chunk, place_ref, both_ref, loss_ref, grad_ref, docs_ref, loss_out, grad_out):
    doc_rows = docs_ref.shape[0] - 2 * recs
    loss, grad = speech_terms(place_ref, chunk, both_ref[...], docs_ref[:doc_rows, :])
    loss_out[...] = loss_ref[...] + loss
    grad_out[...] = grad_ref[...] + grad


def share_kernel(recs, chunk, place_ref, both_ref, loss_ref, grad_ref, *refs):
    blocks, (loss_out, grad_out, send_ref) = refs[:-3], refs[-3:]
    loss, grad = loss_ref[...], grad_ref[...]
    head = []
    if blocks:
        doc_rows = blocks[0].shape[0] - 2 * recs
        more = speech_terms(place_ref, chunk, both_ref[...], blocks[-1][:doc_rows, :])
        loss, grad = loss + more[0], grad + more[1]
        head = [block[doc_rows:, :].astype(f32)[:recs] for block in blocks]
        head = [jnp.concatenate(head + [jnp.zeros_like(head[0])], 0)]
    loss_out[...] = loss[:recs]
    grad_out[...] = grad[:recs]
    loss, grad = loss[recs : 2 * recs], grad[recs : 2 * recs]
    grad_high = grad.astype(bf16).astype(f32)
    loss_high = loss.astype(bf16).astype(f32)
    loss_low = (loss - loss_high).astype(bf16).astype(f32)
    terms = [loss_high, loss_low, loss - loss_high - loss_low]
    terms.append(jnp.zeros((recs, grad.shape[1] - 384), f32))
    send_ref[...] = jnp.concatenate(
        head + [grad_high, grad - grad_high, jnp.concatenate(terms, 1), jnp.zeros_like(grad)], 0
    ).astype(bf16)


def last_kernel(recs, at_ref, docs_ref, loss_ref, grad_ref, came_ref, *refs):
    row_refs, (loss_out, speech_out, doc_out) = refs[:-3], refs[-3:]
    came = came_ref[came_ref.shape[0] - 4 * recs :, :].astype(f32)
    speech_out[...] = grad_ref[...] + came[:recs] + came[recs : 2 * recs]
    terms = came[2 * recs : 3 * recs]
    loss = loss_ref[...] + (terms[:, :128] + terms[:, 128:256] + terms[:, 256:384])
    diagonal = lax.broadcasted_iota(jnp.int32, (recs, 128), 0)
    diagonal = diagonal == lax.broadcasted_iota(jnp.int32, (recs, 128), 1)
    loss_out[...] = jnp.sum(jnp.where(diagonal, loss, 0.0), axis=0, keepdims=True)[:, :recs]
    if len(row_refs) == 1:
        rows = row_refs[0][...]
    else:
        rows = jnp.concatenate([ref[: 4 * recs, :] for ref in row_refs], 0)
    logits = lax.dot_general(docs_ref[...], rows, BY_ROWS, preferred_element_type=f32)
    positive = lax.broadcasted_iota(jnp.int32, logits.shape, 0) == at_ref[:1, : logits.shape[1]]
    _, grad_b = pair_terms(logits, positive)
    doc_out[...] = logit_scale * jnp.dot(grad_b, rows, preferred_element_type=f32)


def swap_pairs(count, stride, steps):
    return [(source, source ^ (steps * stride)) for source in range(count)]


def is_direct(extent):
    return extent <= direct_limit and extent & (extent - 1) == 0


def gathered(value, axis, stride, extent):
    count = lax.axis_size(axis)
    if is_direct(extent):
        parts = [value] + [
            lax.ppermute(value, axis, swap_pairs(count, stride, steps)) for steps in range(1, extent)
        ]
        return parts
    groups = [
        [base + stride * step for step in range(extent)]
        for base in range(count)
        if (base // stride) % extent == 0
    ]
    whole = lax.all_gather(value, axis, axis_index_groups=groups)
    return [whole[step] for step in range(extent)]


def body(features, frame_counts, pool_query, w_proj, doc_embed, doc_index):
    recs, frames, channels = features.shape
    heads, width = pool_query.shape[0], w_proj.shape[1]
    docs_dev = doc_embed.shape[0]
    groups, columns = lax.axis_size("grp"), lax.axis_size("tm")
    layers = groups // 2
    direct = layers == 4
    order = (2, 3, 1) if direct else ()

    def shape(rows, lanes, kind=f32):
        return jax.ShapeDtypeStruct((rows, lanes), kind)

    blocks = []
    if direct:
        blocks = [(0, 0), (0, 1), None, None, *[(n, 0) for n in order], None, *[(n, 1) for n in order]]
    payload, place, at = pl.pallas_call(
        lambda *refs: pool_kernel((docs_dev, is_direct(columns), direct), blocks, *refs),
        out_shape=(
            shape(docs_dev + 4 * recs, width, bf16),
            shape(4 * recs, 128, jnp.int32),
            shape(8, 128, jnp.int32),
        ),
        in_specs=[pl.BlockSpec(memory_space=pltpu.HBM)] * 6,
        out_specs=(VMEM, VMEM, VMEM),
        scratch_shapes=[
            pltpu.SMEM(frame_counts.shape, jnp.int32),
            pltpu.SMEM(doc_index.shape, jnp.int32),
            pltpu.VMEM(pool_query.shape, bf16),
            pltpu.VMEM(features.shape, bf16),
            pltpu.VMEM(w_proj.shape, bf16),
            pltpu.SemaphoreType.DMA((recs + 5,)),
        ],
        compiler_params=pltpu.CompilerParams(vmem_limit_bytes=12 * 2**20),
        name="pool",
    )(
        *[
            pltpu.with_memory_space_constraint(operand, pltpu.HBM)
            for operand in (frame_counts, doc_index, pool_query, features, w_proj, doc_embed)
        ]
    )
    parts = gathered(payload, "tm", 1, columns)
    doc_rows = columns * docs_dev
    own, speech = in_vmem(
        lambda *refs: meet_kernel(recs, heads, *refs),
        (shape(doc_rows + 2 * recs, width, bf16), shape(recs, width, bf16)),
        8,
        "meet",
    )(*parts)

    pairs = swap_pairs(groups, 1, 1)
    other = lax.ppermute(speech, "grp", pairs)
    if direct:
        came = [lax.ppermute(own, "grp", swap_pairs(groups, 2, steps)) for steps in order]
        docs = own
    else:
        came = []
        docs = jnp.concatenate([part[:doc_rows] for part in gathered(own, "grp", 2, layers)] + [own[doc_rows:]])
    mib = 8 + docs.shape[0] // 128
    both, loss, grad = in_vmem(
        lambda *refs: first_docs_kernel(recs, *refs),
        (shape(4 * recs, width, bf16), shape(4 * recs, 128), shape(4 * recs, width)),
        mib,
        "first_docs",
    )(place, own, other, docs)
    for n, block in zip(order[:-1], came[:-1]):
        loss, grad = in_vmem(
            lambda *refs, chunk=n: next_docs_kernel(recs, chunk, *refs),
            (shape(4 * recs, 128), shape(4 * recs, width)),
            8,
            "next_docs",
        )(place, both, loss, grad, block)
    send_rows = 4 * recs * (2 if direct else 1)
    loss, grad, send = in_vmem(
        lambda *refs: share_kernel(recs, order[-1] if order else 0, *refs),
        (shape(recs, 128), shape(recs, width), shape(send_rows, width, bf16)),
        8,
        "share",
    )(place, both, loss, grad, *came)
    back = lax.ppermute(send, "grp", pairs)
    if direct:
        rows = (both, send, back)
    else:
        rows = (lax.all_gather(speech, "grp", tiled=True),)
        at = (doc_index - (lax.axis_index("grp") * columns + lax.axis_index("tm")) * docs_dev)[None, :]
    loss, speech_grad, doc_grad = in_vmem(
        lambda *refs: last_kernel(recs, *refs),
        (shape(1, recs), shape(recs, width), shape(docs_dev, width)),
        8,
        "last",
    )(at, doc_embed, loss, grad, back, *rows)
    return (loss[0], speech_grad, doc_grad)


def solution(mesh):
    placed = (P("grp", "tm", None), P("grp"), P(), P(), P(("grp", "tm"), None), P())
    return jax.shard_map(
        body,
        mesh=mesh,
        in_specs=placed,
        out_specs=(P("grp"), P("grp", None), P(("grp", "tm"), None)),
        check_vma=False,
    )
```

```python
import math

import jax
import jax.numpy as jnp
from jax import lax
from jax.experimental import pallas as pl
from jax.experimental.pallas import tpu as pltpu
from jax.sharding import PartitionSpec as P

logit_scale = 10.0
logit_shift = -8.0
norm_eps = 1e-06
direct_limit = 8
bf16 = jnp.bfloat16
f32 = jnp.float32
BY_ROWS = (((1,), (1,)), ((), ()))
VMEM = pl.BlockSpec(memory_space=pltpu.VMEM)


def in_vmem(kernel, outs, limit_mib, name):
    def call(*operands):
        return pl.pallas_call(
            kernel,
            out_shape=outs,
            in_specs=[VMEM] * len(operands),
            out_specs=jax.tree.map(lambda _: VMEM, outs),
            compiler_params=pltpu.CompilerParams(vmem_limit_bytes=limit_mib * 2**20),
            name=name,
        )(*operands)

    return call


def two_terms(value):
    high = value.astype(bf16)
    return high, (value - high.astype(f32)).astype(bf16)


def pool_kernel(
    scheme,
    blocks,
    counts_hbm,
    index_hbm,
    query_hbm,
    features_hbm,
    proj_hbm,
    docs_hbm,
    out_ref,
    place_ref,
    at_ref,
    counts_ref,
    index_ref,
    query_ref,
    features_ref,
    proj_ref,
    sems,
):
    recs, frames, channels = features_ref.shape
    heads = query_ref.shape[0]
    width = proj_ref.shape[1]
    rows = recs * heads
    docs_dev, by_column, by_layer = scheme
    copies = [
        pltpu.make_async_copy(source, target, sems.at[n])
        for n, (source, target) in enumerate(
            [(counts_hbm, counts_ref), (index_hbm, index_ref), (query_hbm, query_ref)]
            + [(features_hbm.at[r], features_ref.at[r]) for r in range(recs)]
            + [(proj_hbm, proj_ref), (docs_hbm, out_ref.at[:docs_dev])]
        )
    ]
    for copy in copies:
        copy.start()
    copies[1].wait()
    group, column, tm = lax.axis_index("grp"), lax.axis_index("tm"), lax.axis_size("tm")
    layer, core = group // 2, group % 2
    row = lax.broadcasted_iota(jnp.int32, place_ref.shape, 0)
    spot = lax.broadcasted_iota(jnp.int32, place_ref.shape, 1)
    place = jnp.full(place_ref.shape, -1, jnp.int32)
    for r in range(2 * recs):
        target = index_ref[(group ^ (1 - r // recs)) * recs + r % recs]
        of_group, rest = target // (tm * docs_dev), target % (tm * docs_dev)
        of_layer = of_group // 2
        at = (rest // docs_dev) ^ (tm - 1 - column if by_column else 0)
        if by_layer:
            steps = of_layer ^ layer
            far = steps // 2
            at = (at * 2 + far) * docs_dev + rest % docs_dev
            chunk = steps % 2
            mine = (chunk + far + of_group + core) % 2 == 1
        else:
            at = (of_layer * tm + at) * docs_dev + rest % docs_dev
            chunk = 0
            mine = (of_group + core) % 2 == 1
        chunk = jnp.where(mine, chunk, -1)
        place = jnp.where((row == r) & (spot == chunk), at, place)
    place_ref[...] = place
    spot = lax.broadcasted_iota(jnp.int32, at_ref.shape, 1)
    ats = jnp.full(at_ref.shape, -1, jnp.int32)
    first = (group * tm + column) * docs_dev
    for n, block in enumerate(blocks):
        if block is not None:
            base = ((layer ^ block[0]) * 2 + (core ^ block[1])) * recs
            for r in range(recs):
                ats = jnp.where(spot == n * recs + r, index_ref[base + r] - first, ats)
    at_ref[...] = ats
    copies[0].wait()
    copies[2].wait()
    query = jnp.concatenate([query_ref[...].astype(f32), jnp.zeros((128 - heads, channels), f32)], 0).T.astype(bf16)
    start = lax.axis_index("tm") * frames
    spots = lax.broadcasted_iota(jnp.int32, (heads, frames), 1)
    scores, weights, peaks, totals, highs, lows = [], [], [], [], [], []
    for step in range(recs + 2):
        if step < recs:
            copies[3 + step].wait()
            scores.append(
                jnp.dot(features_ref[step], query, preferred_element_type=f32).T[:heads]
            )
        if 0 <= step - 1 < recs:
            r = step - 1
            valid = spots < counts_ref[r] - start
            masked = jnp.where(valid, scores[r] / math.sqrt(channels), -1e30)
            peak = jnp.max(masked, axis=1, keepdims=True).astype(bf16).astype(f32)
            weight = jnp.where(valid, jnp.exp(masked - peak), 0.0)
            peaks.append(peak)
            totals.append(jnp.sum(weight, axis=1, keepdims=True))
            weights.append(jnp.concatenate(two_terms(weight), 0))
        if 0 <= step - 2 < recs:
            r = step - 2
            both = jnp.dot(weights[r], features_ref[r], preferred_element_type=f32)
            high, low = two_terms(both[:heads] + both[heads:])
            highs.append(high)
            lows.append(low)
    peak, totals = jnp.concatenate(peaks, 0), jnp.concatenate(totals, 0)
    copies[3 + recs].wait()
    wide = jnp.dot(jnp.concatenate(highs + lows, 0), proj_ref[...], preferred_element_type=f32)
    wide = wide[:rows] + wide[rows:]
    own = lax.broadcasted_iota(jnp.int32, (rows, width), 1) // (width // heads)
    own = own == lax.broadcasted_iota(jnp.int32, (rows, width), 0) % heads
    lane = lax.broadcasted_iota(jnp.int32, (rows, 128), 1)
    lane = lane == lax.broadcasted_iota(jnp.int32, (rows, 128), 0) % heads

    def over_heads(value):
        return jnp.concatenate(
            [jnp.sum(value[r * heads : (r + 1) * heads], 0, keepdims=True) for r in range(recs)], 0
        )

    pooled = over_heads(jnp.where(own, wide, 0.0))
    pooled_high = pooled.astype(bf16).astype(f32)
    totals = over_heads(jnp.where(lane, totals, 0.0))
    totals_high = totals.astype(bf16).astype(f32)
    peaks = over_heads(jnp.where(lane, peak, 0.0))
    stats = [peaks, totals_high, totals - totals_high, jnp.zeros((recs, width - 384), f32)]
    copies[4 + recs].wait()
    out_ref[docs_dev:, :] = jnp.concatenate(
        [pooled_high, pooled - pooled_high, jnp.concatenate(stats, 1), jnp.zeros((recs, width), f32)], 0
    ).astype(bf16)


def meet_kernel(recs, heads, docs_dev, *refs):
    parts, (send_ref, speech_ref) = refs[:-2], refs[-2:]
    doc_rows = parts[0].shape[0] - 4 * recs
    width = parts[0].shape[1]
    pools = [part[docs_dev : docs_dev + 4 * recs, :].astype(f32) for part in parts]
    peaks = [pool[2 * recs : 3 * recs, :128] for pool in pools]
    totals = [pool[2 * recs : 3 * recs, 128:256] + pool[2 * recs : 3 * recs, 256:384] for pool in pools]
    top = peaks[0]
    for peak in peaks[1:]:
        top = jnp.maximum(top, peak)
    shares = [jnp.exp(peak - top) for peak in peaks]
    whole = shares[0] * totals[0]
    for share, total in zip(shares[1:], totals[1:]):
        whole = whole + share * total
    used = lax.broadcasted_iota(jnp.int32, whole.shape, 1) < heads
    inverse = jnp.where(used, 1.0 / jnp.where(used, whole, 1.0), 0.0)
    high, low = two_terms(jnp.concatenate([share * inverse for share in shares], 0))
    spread = lax.broadcasted_iota(jnp.int32, (128, width), 1) // (width // heads)
    spread = (spread == lax.broadcasted_iota(jnp.int32, (128, width), 0)).astype(f32).astype(bf16)
    scales = jnp.dot(high, spread, preferred_element_type=f32) + jnp.dot(
        low, spread, preferred_element_type=f32
    )
    pooled = jnp.zeros((recs, width), f32)
    for n, pool in enumerate(pools):
        pooled = pooled + (pool[:recs] + pool[recs : 2 * recs]) * scales[n * recs : (n + 1) * recs]
    speech = pooled * lax.rsqrt(jnp.sum(pooled * pooled, axis=1, keepdims=True) + norm_eps)
    speech_ref[...] = speech.astype(bf16)
    for n, part in enumerate(parts):
        send_ref[n * doc_rows : n * doc_rows + docs_dev, :] = part[:docs_dev, :]
        if doc_rows > docs_dev:
            send_ref[n * doc_rows + docs_dev : (n + 1) * doc_rows, :] = part[docs_dev + 4 * recs :, :]
    send_ref[len(parts) * doc_rows :, :] = jnp.concatenate(
        [speech, jnp.zeros((recs, width), f32)], 0
    ).astype(bf16)


def pair_terms(logits, positive):
    logits = logit_scale * logits + logit_shift
    signed = jnp.where(positive, -logits, logits)
    losses = jnp.maximum(signed, 0.0) + jnp.log1p(jnp.exp(-jnp.abs(signed)))
    slopes = jax.nn.sigmoid(signed)
    return losses, jnp.where(positive, -slopes, slopes).astype(bf16)


def speech_terms(place_ref, chunk, speech, docs):
    logits = lax.dot_general(speech, docs, BY_ROWS, preferred_element_type=f32)
    positive = lax.broadcasted_iota(jnp.int32, logits.shape, 1) == place_ref[:, chunk : chunk + 1]
    losses, grad_b = pair_terms(logits, positive)
    grad = logit_scale * jnp.dot(grad_b, docs, preferred_element_type=f32)
    return jnp.sum(losses, axis=1, keepdims=True), grad


def first_docs_kernel(place_ref, both_ref, docs_ref, loss_ref, grad_ref):
    recs = both_ref.shape[0] // 4
    loss, grad = speech_terms(place_ref, 0, both_ref[...], docs_ref[: docs_ref.shape[0] - 2 * recs, :])
    loss_ref[...] = jnp.broadcast_to(loss, loss_ref.shape)
    grad_ref[...] = grad


def share_kernel(place_ref, both_ref, loss_ref, grad_ref, *refs):
    blocks, (loss_out, grad_out, send_ref) = refs[:-3], refs[-3:]
    recs = both_ref.shape[0] // 4
    loss, grad = loss_ref[...], grad_ref[...]
    head = jnp.zeros((recs, grad.shape[1]), f32)
    for block in blocks:
        doc_rows = block.shape[0] - 2 * recs
        more = speech_terms(place_ref, 1, both_ref[...], block[:doc_rows, :])
        loss, grad = loss + more[0], grad + more[1]
        head = block[doc_rows:, :].astype(f32)[:recs]
    loss_out[...] = loss[recs : 2 * recs]
    grad_out[...] = grad[recs : 2 * recs]
    loss, grad = loss[:recs], grad[:recs]
    grad_high = grad.astype(bf16).astype(f32)
    loss_high = loss.astype(bf16).astype(f32)
    loss_low = (loss - loss_high).astype(bf16).astype(f32)
    terms = [loss_high, loss_low, loss - loss_high - loss_low]
    terms.append(jnp.zeros((recs, grad.shape[1] - 384), f32))
    send_ref[...] = jnp.concatenate(
        [head, grad_high, grad - grad_high, jnp.concatenate(terms, 1)], 0
    ).astype(bf16)


def last_kernel(at_ref, docs_ref, loss_ref, grad_ref, back_ref, *refs):
    row_refs, (loss_out, speech_out, doc_out) = refs[:-3], refs[-3:]
    recs = speech_out.shape[0]
    back = back_ref[...].astype(f32)
    speech_out[...] = grad_ref[...] + back[recs : 2 * recs] + back[2 * recs : 3 * recs]
    terms = back[3 * recs :]
    loss = loss_ref[...] + (terms[:, :128] + terms[:, 128:256] + terms[:, 256:384])
    diagonal = lax.broadcasted_iota(jnp.int32, (recs, 128), 0)
    diagonal = diagonal == lax.broadcasted_iota(jnp.int32, (recs, 128), 1)
    loss_out[...] = jnp.sum(jnp.where(diagonal, loss, 0.0), axis=0, keepdims=True)[:, :recs]
    if len(row_refs) == 1:
        rows = row_refs[0][...]
    else:
        both, send, *beyond = [ref[...].astype(f32) for ref in row_refs]
        beyond = [part[: 2 * recs] for part in beyond]
        rows = jnp.concatenate([both, send[:recs], back[:recs], *beyond], 0).astype(bf16)
    logits = lax.dot_general(docs_ref[...], rows, BY_ROWS, preferred_element_type=f32)
    positive = lax.broadcasted_iota(jnp.int32, logits.shape, 0) == at_ref[:1, : logits.shape[1]]
    _, grad_b = pair_terms(logits, positive)
    doc_out[...] = logit_scale * jnp.dot(grad_b, rows, preferred_element_type=f32)


def swap_pairs(count, stride, steps):
    return [(source, source ^ (steps * stride)) for source in range(count)]


def is_direct(extent):
    return extent <= direct_limit and extent & (extent - 1) == 0


def to_other_core(value):
    return lax.ppermute(value, "grp", swap_pairs(lax.axis_size("grp"), 1, 1))


def crossing(value, layer_steps, column_steps):
    columns = lax.axis_size("tm")
    count = lax.axis_size("grp") * columns
    steps = (2 * layer_steps + 1) * columns + column_steps
    return lax.ppermute(value, ("grp", "tm"), swap_pairs(count, 1, steps))


def body(features, frame_counts, pool_query, w_proj, doc_embed, doc_index):
    recs, frames, channels = features.shape
    heads, width = pool_query.shape[0], w_proj.shape[1]
    docs_dev = doc_embed.shape[0]
    groups, columns = lax.axis_size("grp"), lax.axis_size("tm")
    layers = groups // 2
    direct = layers == 4
    order = (3, 2) if direct else ()

    def shape(rows, lanes, kind=f32):
        return jax.ShapeDtypeStruct((rows, lanes), kind)

    blocks = []
    if direct:
        blocks = [(0, 1), (0, 0), None, None, (1, 0), (1, 1)]
        blocks += [(steps, flip) for steps in order for flip in (0, 1)]
        far = crossing(doc_embed, 2, 0)
    payload, place, at = pl.pallas_call(
        lambda *refs: pool_kernel((docs_dev, is_direct(columns), direct), blocks, *refs),
        out_shape=(
            shape(docs_dev + 4 * recs, width, bf16),
            shape(4 * recs, 128, jnp.int32),
            shape(8, 128, jnp.int32),
        ),
        in_specs=[pl.BlockSpec(memory_space=pltpu.HBM)] * 6,
        out_specs=(VMEM, VMEM, VMEM),
        scratch_shapes=[
            pltpu.SMEM(frame_counts.shape, jnp.int32),
            pltpu.SMEM(doc_index.shape, jnp.int32),
            pltpu.VMEM(pool_query.shape, bf16),
            pltpu.VMEM(features.shape, bf16),
            pltpu.VMEM(w_proj.shape, bf16),
            pltpu.SemaphoreType.DMA((recs + 5,)),
        ],
        compiler_params=pltpu.CompilerParams(vmem_limit_bytes=12 * 2**20),
        name="pool",
    )(
        *[
            pltpu.with_memory_space_constraint(operand, pltpu.HBM)
            for operand in (frame_counts, doc_index, pool_query, features, w_proj, doc_embed)
        ]
    )
    if direct:
        payload = jnp.concatenate([payload, far])
    parts = [to_other_core(payload)]
    if is_direct(columns):
        parts = [crossing(payload, 0, steps) for steps in range(columns - 1, 0, -1)] + parts
    else:
        parts = list(lax.all_gather(parts[0], "tm"))
    doc_rows = columns * (payload.shape[0] - 4 * recs)
    own, speech = in_vmem(
        lambda *refs: meet_kernel(recs, heads, docs_dev, *refs),
        (shape(doc_rows + 2 * recs, width, bf16), shape(recs, width, bf16)),
        8,
        "meet",
    )(*parts)

    other = to_other_core(speech)
    chip = jnp.concatenate([speech, other])
    both = jnp.concatenate([chip, jnp.zeros((2 * recs, width), bf16)])
    docs, near = own, []
    if direct:
        near = [crossing(own, 1, 0)]
        beyond = [crossing(both, steps, 0) for steps in order]
    else:
        same_core = [[2 * n + core for n in range(layers)] for core in range(2)]
        docs = lax.all_gather(own[:doc_rows], "grp", axis_index_groups=same_core, tiled=True)
        docs = jnp.concatenate([docs, own[doc_rows:]])
    loss, grad = in_vmem(
        first_docs_kernel,
        (shape(4 * recs, 128), shape(4 * recs, width)),
        8 + docs.shape[0] // 128,
        "first_docs",
    )(place, both, docs)
    loss, grad, send = in_vmem(
        share_kernel,
        (shape(recs, 128), shape(recs, width), shape(4 * recs, width, bf16)),
        8,
        "share",
    )(place, both, loss, grad, *near)
    back = to_other_core(send)
    if direct:
        rows = (both, send, *beyond)
    else:
        rows = (lax.all_gather(speech, "grp", tiled=True),)
        at = doc_index.reshape(layers, 2, recs)[:, ::-1].reshape(1, -1)
        at = at - (lax.axis_index("grp") * columns + lax.axis_index("tm")) * docs_dev
    loss, speech_grad, doc_grad = in_vmem(
        last_kernel,
        (shape(1, recs), shape(recs, width), shape(docs_dev, width)),
        8,
        "last",
    )(at, doc_embed, loss, grad, back, *rows)
    return (loss[0], speech_grad, doc_grad)


def solution(mesh):
    placed = (P("grp", "tm", None), P("grp"), P(), P(), P(("grp", "tm"), None), P())
    return jax.shard_map(
        body,
        mesh=mesh,
        in_specs=placed,
        out_specs=(P("grp"), P("grp", None), P(("grp", "tm"), None)),
        check_vma=False,
    )
```

```python
import math

import jax
import jax.numpy as jnp
from jax import lax
from jax.experimental import pallas as pl
from jax.experimental.pallas import tpu as pltpu
from jax.sharding import PartitionSpec as P

logit_scale = 10.0
logit_shift = -8.0
norm_eps = 1e-06
direct_limit = 8
bf16 = jnp.bfloat16
f32 = jnp.float32
BY_ROWS = (((1,), (1,)), ((), ()))
VMEM = pl.BlockSpec(memory_space=pltpu.VMEM)


def in_vmem(kernel, outs, limit_mib, name):
    def call(*operands):
        return pl.pallas_call(
            kernel,
            out_shape=outs,
            in_specs=[VMEM] * len(operands),
            out_specs=jax.tree.map(lambda _: VMEM, outs),
            compiler_params=pltpu.CompilerParams(vmem_limit_bytes=limit_mib * 2**20),
            name=name,
        )(*operands)

    return call


def two_terms(value):
    high = value.astype(bf16)
    return high, (value - high.astype(f32)).astype(bf16)


def pool_kernel(
    scheme,
    blocks,
    counts_hbm,
    index_hbm,
    query_hbm,
    features_hbm,
    proj_hbm,
    docs_hbm,
    docs_ref,
    out_ref,
    place_ref,
    at_ref,
    counts_ref,
    index_ref,
    query_ref,
    features_ref,
    proj_ref,
    sems,
):
    recs, frames, channels = features_ref.shape
    heads = query_ref.shape[0]
    width = proj_ref.shape[1]
    rows = recs * heads
    docs_dev, by_column, by_layer = scheme
    copies = [
        pltpu.make_async_copy(source, target, sems.at[n])
        for n, (source, target) in enumerate(
            [(counts_hbm, counts_ref), (index_hbm, index_ref), (query_hbm, query_ref)]
            + [(features_hbm.at[r], features_ref.at[r]) for r in range(recs)]
            + [(proj_hbm, proj_ref), (docs_hbm, docs_ref)]
        )
    ]
    for copy in copies:
        copy.start()
    copies[1].wait()
    group, column, tm = lax.axis_index("grp"), lax.axis_index("tm"), lax.axis_size("tm")
    layer, core = group // 2, group % 2
    row = lax.broadcasted_iota(jnp.int32, place_ref.shape, 0)
    spot = lax.broadcasted_iota(jnp.int32, place_ref.shape, 1)
    place = jnp.full(place_ref.shape, -1, jnp.int32)
    for r in range(2 * recs):
        target = index_ref[(group ^ (1 - r // recs)) * recs + r % recs]
        of_group, rest = target // (tm * docs_dev), target % (tm * docs_dev)
        of_layer = of_group // 2
        at = (rest // docs_dev) ^ (column if by_column else 0)
        if by_layer:
            steps = of_layer ^ layer
            far = steps // 2
            at = (at * 2 + far) * docs_dev + rest % docs_dev
            chunk = steps % 2
            mine = (chunk + of_group + core) % 2 == 1
        else:
            at = (of_layer * tm + at) * docs_dev + rest % docs_dev
            chunk = 0
            mine = (of_group + core) % 2 == 1
        chunk = jnp.where(mine, chunk, -1)
        place = jnp.where((row == r) & (spot == chunk), at, place)
    place_ref[...] = place
    spot = lax.broadcasted_iota(jnp.int32, at_ref.shape, 1)
    ats = jnp.full(at_ref.shape, -1, jnp.int32)
    first = (group * tm + column) * docs_dev
    for n, block in enumerate(blocks):
        if block is not None:
            base = ((layer ^ block[0]) * 2 + (core ^ block[1])) * recs
            for r in range(recs):
                ats = jnp.where(spot == n * recs + r, index_ref[base + r] - first, ats)
    at_ref[...] = ats
    copies[0].wait()
    copies[2].wait()
    query = jnp.concatenate([query_ref[...].astype(f32), jnp.zeros((128 - heads, channels), f32)], 0).T.astype(bf16)
    start = lax.axis_index("tm") * frames
    spots = lax.broadcasted_iota(jnp.int32, (heads, frames), 1)
    scores, weights, peaks, totals, highs, lows = [], [], [], [], [], []
    for step in range(recs + 2):
        if step < recs:
            copies[3 + step].wait()
            scores.append(
                jnp.dot(features_ref[step], query, preferred_element_type=f32).T[:heads]
            )
        if 0 <= step - 1 < recs:
            r = step - 1
            valid = spots < counts_ref[r] - start
            masked = jnp.where(valid, scores[r] / math.sqrt(channels), -1e30)
            peak = jnp.max(masked, axis=1, keepdims=True).astype(bf16).astype(f32)
            weight = jnp.where(valid, jnp.exp(masked - peak), 0.0)
            peaks.append(peak)
            totals.append(jnp.sum(weight, axis=1, keepdims=True))
            weights.append(jnp.concatenate(two_terms(weight), 0))
        if 0 <= step - 2 < recs:
            r = step - 2
            both = jnp.dot(weights[r], features_ref[r], preferred_element_type=f32)
            high, low = two_terms(both[:heads] + both[heads:])
            highs.append(high)
            lows.append(low)
    peak, totals = jnp.concatenate(peaks, 0), jnp.concatenate(totals, 0)
    copies[3 + recs].wait()
    wide = jnp.dot(jnp.concatenate(highs + lows, 0), proj_ref[...], preferred_element_type=f32)
    wide = wide[:rows] + wide[rows:]
    own = lax.broadcasted_iota(jnp.int32, (rows, width), 1) // (width // heads)
    own = own == lax.broadcasted_iota(jnp.int32, (rows, width), 0) % heads
    lane = lax.broadcasted_iota(jnp.int32, (rows, 128), 1)
    lane = lane == lax.broadcasted_iota(jnp.int32, (rows, 128), 0) % heads

    def over_heads(value):
        return jnp.concatenate(
            [jnp.sum(value[r * heads : (r + 1) * heads], 0, keepdims=True) for r in range(recs)], 0
        )

    pooled = over_heads(jnp.where(own, wide, 0.0))
    pooled_high = pooled.astype(bf16).astype(f32)
    totals = over_heads(jnp.where(lane, totals, 0.0))
    totals_high = totals.astype(bf16).astype(f32)
    peaks = over_heads(jnp.where(lane, peak, 0.0))
    stats = [peaks, totals_high, totals - totals_high, jnp.zeros((recs, width - 384), f32)]
    copies[4 + recs].wait()
    out_ref[...] = jnp.concatenate(
        [pooled_high, pooled - pooled_high, jnp.concatenate(stats, 1), jnp.zeros((recs, width), f32)], 0
    ).astype(bf16)


def meet_kernel(recs, heads, doc_rows, apart, *refs):
    parts, (send_ref, both_ref) = list(refs[:-2]), refs[-2:]
    width = parts[0].shape[1]
    last = [parts.pop(), parts.pop()][::-1] if apart else []
    sums, peaks, totals = [], [], []
    for part in parts:
        pool = part[doc_rows:, :].astype(f32)
        sums.append([pool[n : n + recs] + pool[n + recs : n + 2 * recs] for n in (0, 2 * recs)])
        peaks.append(pool[4 * recs :, :128])
        totals.append(pool[4 * recs :, 128:256] + pool[4 * recs :, 256:384])
    if apart:
        pools = [part[part.shape[0] - 4 * recs :, :].astype(f32) for part in last]
        sums.append([pool[:recs] + pool[recs : 2 * recs] for pool in pools])
        stats = jnp.concatenate([pool[2 * recs : 3 * recs] for pool in pools], 0)
        peaks.append(stats[:, :128])
        totals.append(stats[:, 128:256] + stats[:, 256:384])
        parts.append(last[0])
    sums = [jnp.concatenate(pair, 0) for pair in sums]
    top = peaks[0]
    for peak in peaks[1:]:
        top = jnp.maximum(top, peak)
    shares = [jnp.exp(peak - top) for peak in peaks]
    whole = shares[0] * totals[0]
    for share, total in zip(shares[1:], totals[1:]):
        whole = whole + share * total
    used = lax.broadcasted_iota(jnp.int32, whole.shape, 1) < heads
    inverse = jnp.where(used, 1.0 / jnp.where(used, whole, 1.0), 0.0)
    high, low = two_terms(jnp.concatenate([share * inverse for share in shares], 0))
    spread = lax.broadcasted_iota(jnp.int32, (128, width), 1) // (width // heads)
    spread = (spread == lax.broadcasted_iota(jnp.int32, (128, width), 0)).astype(f32).astype(bf16)
    scales = jnp.dot(high, spread, preferred_element_type=f32) + jnp.dot(
        low, spread, preferred_element_type=f32
    )
    pooled = jnp.zeros((2 * recs, width), f32)
    for n, part in enumerate(sums):
        pooled = pooled + part * scales[2 * n * recs : 2 * (n + 1) * recs]
    speech = pooled * lax.rsqrt(jnp.sum(pooled * pooled, axis=1, keepdims=True) + norm_eps)
    both_ref[...] = jnp.concatenate([speech, jnp.zeros((2 * recs, width), f32)], 0).astype(bf16)
    for n, part in enumerate(parts):
        send_ref[n * doc_rows : (n + 1) * doc_rows, :] = part[:doc_rows, :]
    send_ref[len(parts) * doc_rows :, :] = speech.astype(bf16)


def pair_terms(logits, positive):
    logits = logit_scale * logits + logit_shift
    signed = jnp.where(positive, -logits, logits)
    losses = jnp.maximum(signed, 0.0) + jnp.log1p(jnp.exp(-jnp.abs(signed)))
    slopes = jax.nn.sigmoid(signed)
    return losses, jnp.where(positive, -slopes, slopes).astype(bf16)


def speech_terms(place_ref, chunk, speech, docs):
    logits = lax.dot_general(speech, docs, BY_ROWS, preferred_element_type=f32)
    positive = lax.broadcasted_iota(jnp.int32, logits.shape, 1) == place_ref[:, chunk : chunk + 1]
    losses, grad_b = pair_terms(logits, positive)
    grad = logit_scale * jnp.dot(grad_b, docs, preferred_element_type=f32)
    return jnp.sum(losses, axis=1, keepdims=True), grad


def first_docs_kernel(place_ref, both_ref, docs_ref, loss_ref, grad_ref):
    recs = both_ref.shape[0] // 4
    loss, grad = speech_terms(place_ref, 0, both_ref[...], docs_ref[: docs_ref.shape[0] - 2 * recs, :])
    loss_ref[...] = jnp.broadcast_to(loss, loss_ref.shape)
    grad_ref[...] = grad


def share_kernel(place_ref, both_ref, loss_ref, grad_ref, *refs):
    blocks, (loss_out, grad_out, send_ref) = refs[:-3], refs[-3:]
    recs = both_ref.shape[0] // 4
    loss, grad = loss_ref[...], grad_ref[...]
    for block in blocks:
        doc_rows = block.shape[0] - 2 * recs
        more = speech_terms(place_ref, 1, both_ref[...], block[:doc_rows, :])
        loss, grad = loss + more[0], grad + more[1]
    loss_out[...] = loss[recs : 2 * recs]
    grad_out[...] = grad[recs : 2 * recs]
    loss, grad = loss[:recs], grad[:recs]
    grad_high = grad.astype(bf16).astype(f32)
    loss_high = loss.astype(bf16).astype(f32)
    loss_low = (loss - loss_high).astype(bf16).astype(f32)
    terms = [loss_high, loss_low, loss - loss_high - loss_low]
    terms.append(jnp.zeros((recs, grad.shape[1] - 384), f32))
    send_ref[...] = jnp.concatenate(
        [grad_high, grad - grad_high, jnp.concatenate(terms, 1), jnp.zeros_like(grad)], 0
    ).astype(bf16)


def last_kernel(at_ref, docs_ref, loss_ref, grad_ref, back_ref, *refs):
    row_refs, (loss_out, speech_out, doc_out) = refs[:-3], refs[-3:]
    recs = speech_out.shape[0]
    back = back_ref[...].astype(f32)
    speech_out[...] = grad_ref[...] + back[:recs] + back[recs : 2 * recs]
    terms = back[2 * recs : 3 * recs]
    loss = loss_ref[...] + (terms[:, :128] + terms[:, 128:256] + terms[:, 256:384])
    diagonal = lax.broadcasted_iota(jnp.int32, (recs, 128), 0)
    diagonal = diagonal == lax.broadcasted_iota(jnp.int32, (recs, 128), 1)
    loss_out[...] = jnp.sum(jnp.where(diagonal, loss, 0.0), axis=0, keepdims=True)[:, :recs]
    if len(row_refs) == 1:
        rows = row_refs[0][...]
    else:
        both, near, *beyond = row_refs
        near = near[near.shape[0] - 2 * recs :, :].astype(f32)
        beyond = [ref[...].astype(f32)[: 2 * recs] for ref in beyond]
        rows = jnp.concatenate([both[...].astype(f32), near, *beyond], 0).astype(bf16)
    logits = lax.dot_general(docs_ref[...], rows, BY_ROWS, preferred_element_type=f32)
    positive = lax.broadcasted_iota(jnp.int32, logits.shape, 0) == at_ref[:1, : logits.shape[1]]
    _, grad_b = pair_terms(logits, positive)
    doc_out[...] = logit_scale * jnp.dot(grad_b, rows, preferred_element_type=f32)


def swap_pairs(count, stride, steps):
    return [(source, source ^ (steps * stride)) for source in range(count)]


def is_direct(extent):
    return extent <= direct_limit and extent & (extent - 1) == 0


def to_other_core(value):
    return lax.ppermute(value, "grp", swap_pairs(lax.axis_size("grp"), 1, 1))


def crossing(value, layer_steps, column_steps):
    columns = lax.axis_size("tm")
    count = lax.axis_size("grp") * columns
    steps = (2 * layer_steps + 1) * columns + column_steps
    return lax.ppermute(value, ("grp", "tm"), swap_pairs(count, 1, steps))


def body(features, frame_counts, pool_query, w_proj, doc_embed, doc_index):
    recs, frames, channels = features.shape
    heads, width = pool_query.shape[0], w_proj.shape[1]
    docs_dev = doc_embed.shape[0]
    groups, columns = lax.axis_size("grp"), lax.axis_size("tm")
    layers = groups // 2
    direct = layers == 4
    order = (2, 3) if direct else ()

    def shape(rows, lanes, kind=f32):
        return jax.ShapeDtypeStruct((rows, lanes), kind)

    blocks = []
    if direct:
        blocks = [(0, 1), (0, 0), None, None, (1, 0), (1, 1)]
        blocks += [(steps, flip) for steps in order for flip in (0, 1)]
        far = lax.ppermute(doc_embed, "grp", swap_pairs(groups, 2, 2))
    docs, pools, place, at = pl.pallas_call(
        lambda *refs: pool_kernel((docs_dev, is_direct(columns), direct), blocks, *refs),
        out_shape=(
            shape(docs_dev, width, bf16),
            shape(4 * recs, width, bf16),
            shape(4 * recs, 128, jnp.int32),
            shape(8, 128, jnp.int32),
        ),
        in_specs=[pl.BlockSpec(memory_space=pltpu.HBM)] * 6,
        out_specs=(VMEM,) * 4,
        scratch_shapes=[
            pltpu.SMEM(frame_counts.shape, jnp.int32),
            pltpu.SMEM(doc_index.shape, jnp.int32),
            pltpu.VMEM(pool_query.shape, bf16),
            pltpu.VMEM(features.shape, bf16),
            pltpu.VMEM(w_proj.shape, bf16),
            pltpu.SemaphoreType.DMA((recs + 5,)),
        ],
        compiler_params=pltpu.CompilerParams(vmem_limit_bytes=12 * 2**20),
        name="pool",
    )(
        *[
            pltpu.with_memory_space_constraint(operand, pltpu.HBM)
            for operand in (frame_counts, doc_index, pool_query, features, w_proj, doc_embed)
        ]
    )
    other = to_other_core(pools)
    docs = [docs, *([far] if direct else [])]
    payload = [pools[: 2 * recs], other[: 2 * recs], pools[2 * recs : 3 * recs], other[2 * recs : 3 * recs]]
    payload = jnp.concatenate([*docs, *payload])
    parts = [to_other_core(payload)]
    doc_rows = columns * (payload.shape[0] - 6 * recs)
    if is_direct(columns):
        parts += [crossing(payload, 0, steps) for steps in range(1, columns - 1)]
        parts.append(crossing(jnp.concatenate([*docs, pools]), 0, columns - 1))
        parts.append(to_other_core(parts[-1][doc_rows // columns :]))
    else:
        parts = list(lax.all_gather(parts[0], "tm"))
    own, both = in_vmem(
        lambda *refs: meet_kernel(recs, heads, doc_rows // columns, is_direct(columns), *refs),
        (shape(doc_rows + 2 * recs, width, bf16), shape(4 * recs, width, bf16)),
        8,
        "meet",
    )(*parts)

    docs, near = own, []
    if direct:
        near = [crossing(own, 1, 0)]
        beyond = [crossing(both, steps, 0) for steps in order]
    else:
        same_core = [[2 * n + core for n in range(layers)] for core in range(2)]
        docs = lax.all_gather(own[:doc_rows], "grp", axis_index_groups=same_core, tiled=True)
        docs = jnp.concatenate([docs, own[doc_rows:]])
    loss, grad = in_vmem(
        first_docs_kernel,
        (shape(4 * recs, 128), shape(4 * recs, width)),
        8 + docs.shape[0] // 128,
        "first_docs",
    )(place, both, docs)
    loss, grad, send = in_vmem(
        share_kernel,
        (shape(recs, 128), shape(recs, width), shape(4 * recs, width, bf16)),
        8,
        "share",
    )(place, both, loss, grad, *near)
    back = to_other_core(send)
    if direct:
        rows = (both, *near, *beyond)
    else:
        rows = (lax.all_gather(both[:recs], "grp", tiled=True),)
        at = doc_index.reshape(layers, 2, recs)[:, ::-1].reshape(1, -1)
        at = at - (lax.axis_index("grp") * columns + lax.axis_index("tm")) * docs_dev
    loss, speech_grad, doc_grad = in_vmem(
        last_kernel,
        (shape(1, recs), shape(recs, width), shape(docs_dev, width)),
        8,
        "last",
    )(at, doc_embed, loss, grad, back, *rows)
    return (loss[0], speech_grad, doc_grad)


def solution(mesh):
    placed = (P("grp", "tm", None), P("grp"), P(), P(), P(("grp", "tm"), None), P())
    return jax.shard_map(
        body,
        mesh=mesh,
        in_specs=placed,
        out_specs=(P("grp"), P("grp", None), P(("grp", "tm"), None)),
        check_vma=False,
    )
```

```python
import math

import jax
import jax.numpy as jnp
from jax import lax
from jax.experimental import pallas as pl
from jax.experimental.pallas import tpu as pltpu
from jax.sharding import PartitionSpec as P

logit_scale = 10.0
logit_shift = -8.0
norm_eps = 1e-06
direct_limit = 8
bf16 = jnp.bfloat16
f32 = jnp.float32
BY_ROWS = (((1,), (1,)), ((), ()))
VMEM = pl.BlockSpec(memory_space=pltpu.VMEM)


def in_vmem(kernel, outs, limit_mib, name):
    def call(*operands):
        return pl.pallas_call(
            kernel,
            out_shape=outs,
            in_specs=[VMEM] * len(operands),
            out_specs=jax.tree.map(lambda _: VMEM, outs),
            compiler_params=pltpu.CompilerParams(vmem_limit_bytes=limit_mib * 2**20),
            name=name,
        )(*operands)

    return call


def two_terms(value):
    high = value.astype(bf16)
    return high, (value - high.astype(f32)).astype(bf16)


def pool_kernel(
    scheme,
    blocks,
    counts_hbm,
    index_hbm,
    query_hbm,
    features_hbm,
    proj_hbm,
    docs_hbm,
    docs_ref,
    out_ref,
    place_ref,
    at_ref,
    counts_ref,
    index_ref,
    query_ref,
    features_ref,
    proj_ref,
    sems,
):
    recs, frames, channels = features_ref.shape
    heads = query_ref.shape[0]
    width = proj_ref.shape[1]
    rows = recs * heads
    docs_dev, by_column, by_layer = scheme
    copies = [
        pltpu.make_async_copy(source, target, sems.at[n])
        for n, (source, target) in enumerate(
            [(counts_hbm, counts_ref), (index_hbm, index_ref), (query_hbm, query_ref)]
            + [(features_hbm.at[r], features_ref.at[r]) for r in range(recs)]
            + [(proj_hbm, proj_ref), (docs_hbm, docs_ref)]
        )
    ]
    for copy in copies:
        copy.start()
    copies[1].wait()
    group, column, tm = lax.axis_index("grp"), lax.axis_index("tm"), lax.axis_size("tm")
    layer, core = group // 2, group % 2
    row = lax.broadcasted_iota(jnp.int32, place_ref.shape, 0)
    spot = lax.broadcasted_iota(jnp.int32, place_ref.shape, 1)
    place = jnp.full(place_ref.shape, -1, jnp.int32)
    for r in range(2 * recs):
        target = index_ref[(group ^ (r // recs)) * recs + r % recs]
        of_group, rest = target // (tm * docs_dev), target % (tm * docs_dev)
        of_layer = of_group // 2
        at = (rest // docs_dev) ^ (column if by_column else 0)
        if by_layer:
            steps = of_layer ^ layer
            far = steps // 2
            at = (at * 2 + far) * docs_dev + rest % docs_dev
            chunk = steps % 2
            mine = (of_group + core) % 2 == 0
        else:
            at = (of_layer * tm + at) * docs_dev + rest % docs_dev
            chunk = 0
            mine = (of_group + core) % 2 == 0
        chunk = jnp.where(mine, chunk, -1)
        place = jnp.where((row == r) & (spot == chunk), at, place)
    place_ref[...] = place
    spot = lax.broadcasted_iota(jnp.int32, at_ref.shape, 1)
    ats = jnp.full(at_ref.shape, -1, jnp.int32)
    first = (group * tm + column) * docs_dev
    for n, block in enumerate(blocks):
        if block is not None:
            base = ((layer ^ block[0]) * 2 + (core ^ block[1])) * recs
            for r in range(recs):
                ats = jnp.where(spot == n * recs + r, index_ref[base + r] - first, ats)
    at_ref[...] = ats
    copies[0].wait()
    copies[2].wait()
    query = jnp.concatenate([query_ref[...].astype(f32), jnp.zeros((128 - heads, channels), f32)], 0).T.astype(bf16)
    start = lax.axis_index("tm") * frames
    spots = lax.broadcasted_iota(jnp.int32, (heads, frames), 1)
    scores, weights, peaks, totals, highs, lows = [], [], [], [], [], []
    for step in range(recs + 2):
        if step < recs:
            copies[3 + step].wait()
            scores.append(
                jnp.dot(features_ref[step], query, preferred_element_type=f32).T[:heads]
            )
        if 0 <= step - 1 < recs:
            r = step - 1
            valid = spots < counts_ref[r] - start
            masked = jnp.where(valid, scores[r] / math.sqrt(channels), -1e30)
            peak = jnp.max(masked, axis=1, keepdims=True).astype(bf16).astype(f32)
            weight = jnp.where(valid, jnp.exp(masked - peak), 0.0)
            peaks.append(peak)
            totals.append(jnp.sum(weight, axis=1, keepdims=True))
            weights.append(jnp.concatenate(two_terms(weight), 0))
        if 0 <= step - 2 < recs:
            r = step - 2
            both = jnp.dot(weights[r], features_ref[r], preferred_element_type=f32)
            high, low = two_terms(both[:heads] + both[heads:])
            highs.append(high)
            lows.append(low)
    peak, totals = jnp.concatenate(peaks, 0), jnp.concatenate(totals, 0)
    copies[3 + recs].wait()
    wide = jnp.dot(jnp.concatenate(highs + lows, 0), proj_ref[...], preferred_element_type=f32)
    wide = wide[:rows] + wide[rows:]
    own = lax.broadcasted_iota(jnp.int32, (rows, width), 1) // (width // heads)
    own = own == lax.broadcasted_iota(jnp.int32, (rows, width), 0) % heads
    lane = lax.broadcasted_iota(jnp.int32, (rows, 128), 1)
    lane = lane == lax.broadcasted_iota(jnp.int32, (rows, 128), 0) % heads

    def over_heads(value):
        return jnp.concatenate(
            [jnp.sum(value[r * heads : (r + 1) * heads], 0, keepdims=True) for r in range(recs)], 0
        )

    pooled = over_heads(jnp.where(own, wide, 0.0))
    pooled_high = pooled.astype(bf16).astype(f32)
    totals = over_heads(jnp.where(lane, totals, 0.0))
    totals_high = totals.astype(bf16).astype(f32)
    peaks = over_heads(jnp.where(lane, peak, 0.0))
    stats = [peaks, totals_high, totals - totals_high, jnp.zeros((recs, width - 384), f32)]
    copies[4 + recs].wait()
    out_ref[...] = jnp.concatenate(
        [pooled_high, pooled - pooled_high, jnp.concatenate(stats, 1), jnp.zeros((recs, width), f32)], 0
    ).astype(bf16)


def meet_kernel(recs, heads, doc_rows, apart, *refs):
    parts, (send_ref, both_ref) = list(refs[:-2]), refs[-2:]
    width = parts[0].shape[1]
    last = [parts.pop(), parts.pop()][::-1] if apart else []
    sums, peaks, totals = [], [], []
    for part in parts:
        pool = part[doc_rows:, :].astype(f32)
        sums.append([pool[n : n + recs] + pool[n + recs : n + 2 * recs] for n in (0, 2 * recs)])
        peaks.append(pool[4 * recs :, :128])
        totals.append(pool[4 * recs :, 128:256] + pool[4 * recs :, 256:384])
    if apart:
        pools = [part[part.shape[0] - 4 * recs :, :].astype(f32) for part in last]
        sums.append([pool[:recs] + pool[recs : 2 * recs] for pool in pools])
        stats = jnp.concatenate([pool[2 * recs : 3 * recs] for pool in pools], 0)
        peaks.append(stats[:, :128])
        totals.append(stats[:, 128:256] + stats[:, 256:384])
        parts.append(last[0])
    sums = [jnp.concatenate(pair, 0) for pair in sums]
    top = peaks[0]
    for peak in peaks[1:]:
        top = jnp.maximum(top, peak)
    shares = [jnp.exp(peak - top) for peak in peaks]
    whole = shares[0] * totals[0]
    for share, total in zip(shares[1:], totals[1:]):
        whole = whole + share * total
    used = lax.broadcasted_iota(jnp.int32, whole.shape, 1) < heads
    inverse = jnp.where(used, 1.0 / jnp.where(used, whole, 1.0), 0.0)
    high, low = two_terms(jnp.concatenate([share * inverse for share in shares], 0))
    spread = lax.broadcasted_iota(jnp.int32, (128, width), 1) // (width // heads)
    spread = (spread == lax.broadcasted_iota(jnp.int32, (128, width), 0)).astype(f32).astype(bf16)
    scales = jnp.dot(high, spread, preferred_element_type=f32) + jnp.dot(
        low, spread, preferred_element_type=f32
    )
    pooled = jnp.zeros((2 * recs, width), f32)
    for n, part in enumerate(sums):
        pooled = pooled + part * scales[2 * n * recs : 2 * (n + 1) * recs]
    speech = pooled * lax.rsqrt(jnp.sum(pooled * pooled, axis=1, keepdims=True) + norm_eps)
    both_ref[...] = jnp.concatenate([speech, jnp.zeros((2 * recs, width), f32)], 0).astype(bf16)
    for n, part in enumerate(parts):
        send_ref[n * doc_rows : (n + 1) * doc_rows, :] = part[:doc_rows, :]
    send_ref[len(parts) * doc_rows :, :] = speech.astype(bf16)


def pair_terms(logits, positive):
    logits = logit_scale * logits + logit_shift
    signed = jnp.where(positive, -logits, logits)
    losses = jnp.maximum(signed, 0.0) + jnp.log1p(jnp.exp(-jnp.abs(signed)))
    slopes = jax.nn.sigmoid(signed)
    return losses, jnp.where(positive, -slopes, slopes).astype(bf16)


def speech_terms(place_ref, chunk, speech, docs):
    logits = lax.dot_general(speech, docs, BY_ROWS, preferred_element_type=f32)
    positive = lax.broadcasted_iota(jnp.int32, logits.shape, 1) == place_ref[:, chunk : chunk + 1]
    losses, grad_b = pair_terms(logits, positive)
    grad = logit_scale * jnp.dot(grad_b, docs, preferred_element_type=f32)
    return jnp.sum(losses, axis=1, keepdims=True), grad


def first_docs_kernel(place_ref, both_ref, docs_ref, loss_ref, grad_ref):
    recs = both_ref.shape[0] // 4
    loss, grad = speech_terms(place_ref, 0, both_ref[...], docs_ref[: docs_ref.shape[0] - 2 * recs, :])
    loss_ref[...] = jnp.broadcast_to(loss, loss_ref.shape)
    grad_ref[...] = grad


def share_kernel(place_ref, both_ref, loss_ref, grad_ref, *refs):
    blocks, (loss_out, grad_out, send_ref) = refs[:-3], refs[-3:]
    recs = both_ref.shape[0] // 4
    loss, grad = loss_ref[...], grad_ref[...]
    for block in blocks:
        doc_rows = block.shape[0] - 2 * recs
        more = speech_terms(place_ref, 1, both_ref[...], block[:doc_rows, :])
        loss, grad = loss + more[0], grad + more[1]
    loss_out[...] = loss[:recs]
    grad_out[...] = grad[:recs]
    loss, grad = loss[recs : 2 * recs], grad[recs : 2 * recs]
    grad_high = grad.astype(bf16).astype(f32)
    loss_high = loss.astype(bf16).astype(f32)
    loss_low = (loss - loss_high).astype(bf16).astype(f32)
    terms = [loss_high, loss_low, loss - loss_high - loss_low]
    terms.append(jnp.zeros((recs, grad.shape[1] - 384), f32))
    send_ref[...] = jnp.concatenate(
        [grad_high, grad - grad_high, jnp.concatenate(terms, 1), jnp.zeros_like(grad)], 0
    ).astype(bf16)


def last_kernel(at_ref, docs_ref, loss_ref, grad_ref, back_ref, *refs):
    row_refs, (loss_out, speech_out, doc_out) = refs[:-3], refs[-3:]
    recs = speech_out.shape[0]
    back = back_ref[...].astype(f32)
    speech_out[...] = grad_ref[...] + back[:recs] + back[recs : 2 * recs]
    terms = back[2 * recs : 3 * recs]
    loss = loss_ref[...] + (terms[:, :128] + terms[:, 128:256] + terms[:, 256:384])
    diagonal = lax.broadcasted_iota(jnp.int32, (recs, 128), 0)
    diagonal = diagonal == lax.broadcasted_iota(jnp.int32, (recs, 128), 1)
    loss_out[...] = jnp.sum(jnp.where(diagonal, loss, 0.0), axis=0, keepdims=True)[:, :recs]
    if len(row_refs) == 1:
        rows = row_refs[0][...]
    else:
        both, near, *beyond = row_refs
        near = near[near.shape[0] - 2 * recs :, :].astype(f32)
        beyond = [ref[...].astype(f32)[: 2 * recs] for ref in beyond]
        rows = jnp.concatenate([both[...].astype(f32), near, *beyond], 0).astype(bf16)
    logits = lax.dot_general(docs_ref[...], rows, BY_ROWS, preferred_element_type=f32)
    positive = lax.broadcasted_iota(jnp.int32, logits.shape, 0) == at_ref[:1, : logits.shape[1]]
    _, grad_b = pair_terms(logits, positive)
    doc_out[...] = logit_scale * jnp.dot(grad_b, rows, preferred_element_type=f32)


def swap_pairs(count, stride, steps):
    return [(source, source ^ (steps * stride)) for source in range(count)]


def is_direct(extent):
    return extent <= direct_limit and extent & (extent - 1) == 0


def to_other_core(value):
    return lax.ppermute(value, "grp", swap_pairs(lax.axis_size("grp"), 1, 1))


def across(value, layer_steps, column_steps, core_steps=0):
    columns = lax.axis_size("tm")
    steps = (2 * layer_steps + core_steps) * columns + column_steps
    return lax.ppermute(value, ("grp", "tm"), swap_pairs(lax.axis_size("grp") * columns, 1, steps))


def body(features, frame_counts, pool_query, w_proj, doc_embed, doc_index):
    recs, frames, channels = features.shape
    heads, width = pool_query.shape[0], w_proj.shape[1]
    docs_dev = doc_embed.shape[0]
    groups, columns = lax.axis_size("grp"), lax.axis_size("tm")
    layers = groups // 2
    direct = layers == 4
    order = (2, 3) if direct else ()

    def shape(rows, lanes, kind=f32):
        return jax.ShapeDtypeStruct((rows, lanes), kind)

    blocks = []
    if direct:
        blocks = [(0, 0), (0, 1), None, None, (1, 0), (1, 1)]
        blocks += [(steps, flip) for steps in order for flip in (1, 0)]
        far = across(doc_embed, 2, 0)
    docs, pools, place, at = pl.pallas_call(
        lambda *refs: pool_kernel((docs_dev, is_direct(columns), direct), blocks, *refs),
        out_shape=(
            shape(docs_dev, width, bf16),
            shape(4 * recs, width, bf16),
            shape(4 * recs, 128, jnp.int32),
            shape(8, 128, jnp.int32),
        ),
        in_specs=[pl.BlockSpec(memory_space=pltpu.HBM)] * 6,
        out_specs=(VMEM,) * 4,
        scratch_shapes=[
            pltpu.SMEM(frame_counts.shape, jnp.int32),
            pltpu.SMEM(doc_index.shape, jnp.int32),
            pltpu.VMEM(pool_query.shape, bf16),
            pltpu.VMEM(features.shape, bf16),
            pltpu.VMEM(w_proj.shape, bf16),
            pltpu.SemaphoreType.DMA((recs + 5,)),
        ],
        compiler_params=pltpu.CompilerParams(vmem_limit_bytes=12 * 2**20),
        name="pool",
    )(
        *[
            pltpu.with_memory_space_constraint(operand, pltpu.HBM)
            for operand in (frame_counts, doc_index, pool_query, features, w_proj, doc_embed)
        ]
    )
    other = to_other_core(pools)
    docs = [docs, *([far] if direct else [])]
    payload = [pools[: 2 * recs], other[: 2 * recs], pools[2 * recs : 3 * recs], other[2 * recs : 3 * recs]]
    payload = jnp.concatenate([*docs, *payload])
    parts = [payload]
    doc_rows = columns * (payload.shape[0] - 6 * recs)
    if is_direct(columns):
        parts += [across(payload, 0, steps) for steps in range(1, columns - 1)]
        parts.append(across(jnp.concatenate([*docs, pools]), 0, columns - 1))
        parts.append(to_other_core(parts[-1][doc_rows // columns :]))
    else:
        parts = list(lax.all_gather(payload, "tm"))
    own, both = in_vmem(
        lambda *refs: meet_kernel(recs, heads, doc_rows // columns, is_direct(columns), *refs),
        (shape(doc_rows + 2 * recs, width, bf16), shape(4 * recs, width, bf16)),
        8,
        "meet",
    )(*parts)

    docs, near = own, []
    if direct:
        near = [across(own, 1, 0)]
        beyond = [across(both, steps, 0, 1) for steps in order]
    else:
        same_core = [[2 * n + core for n in range(layers)] for core in range(2)]
        docs = lax.all_gather(own[:doc_rows], "grp", axis_index_groups=same_core, tiled=True)
        docs = jnp.concatenate([docs, own[doc_rows:]])
    loss, grad = in_vmem(
        first_docs_kernel,
        (shape(4 * recs, 128), shape(4 * recs, width)),
        8 + docs.shape[0] // 128,
        "first_docs",
    )(place, both, docs)
    loss, grad, send = in_vmem(
        share_kernel,
        (shape(recs, 128), shape(recs, width), shape(4 * recs, width, bf16)),
        8,
        "share",
    )(place, both, loss, grad, *near)
    back = to_other_core(send)
    if direct:
        rows = (both, *near, *beyond)
    else:
        rows = (lax.all_gather(both[:recs], "grp", tiled=True),)
        at = doc_index[None, :] - (lax.axis_index("grp") * columns + lax.axis_index("tm")) * docs_dev
    loss, speech_grad, doc_grad = in_vmem(
        last_kernel,
        (shape(1, recs), shape(recs, width), shape(docs_dev, width)),
        8,
        "last",
    )(at, doc_embed, loss, grad, back, *rows)
    return (loss[0], speech_grad, doc_grad)


def solution(mesh):
    placed = (P("grp", "tm", None), P("grp"), P(), P(), P(("grp", "tm"), None), P())
    return jax.shard_map(
        body,
        mesh=mesh,
        in_specs=placed,
        out_specs=(P("grp"), P("grp", None), P(("grp", "tm"), None)),
        check_vma=False,
    )
```

```python
import math

import jax
import jax.numpy as jnp
from jax import lax
from jax.experimental import pallas as pl
from jax.experimental.pallas import tpu as pltpu
from jax.sharding import PartitionSpec as P

logit_scale = 10.0
logit_shift = -8.0
norm_eps = 1e-06
direct_limit = 8
bf16 = jnp.bfloat16
f32 = jnp.float32
BY_ROWS = (((1,), (1,)), ((), ()))
VMEM = pl.BlockSpec(memory_space=pltpu.VMEM)


def in_vmem(kernel, outs, limit_mib, name):
    def call(*operands):
        return pl.pallas_call(
            kernel,
            out_shape=outs,
            in_specs=[VMEM] * len(operands),
            out_specs=jax.tree.map(lambda _: VMEM, outs),
            compiler_params=pltpu.CompilerParams(vmem_limit_bytes=limit_mib * 2**20),
            name=name,
        )(*operands)

    return call


def two_terms(value):
    high = value.astype(bf16)
    return high, (value - high.astype(f32)).astype(bf16)


def pool_kernel(
    scheme,
    blocks,
    counts_hbm,
    index_hbm,
    query_hbm,
    features_hbm,
    proj_hbm,
    docs_hbm,
    docs_ref,
    out_ref,
    place_ref,
    at_ref,
    counts_ref,
    index_ref,
    query_ref,
    features_ref,
    proj_ref,
    sems,
):
    recs, frames, channels = features_ref.shape
    heads = query_ref.shape[0]
    width = proj_ref.shape[1]
    rows = recs * heads
    docs_dev, by_column, by_layer = scheme
    copies = [
        pltpu.make_async_copy(source, target, sems.at[n])
        for n, (source, target) in enumerate(
            [(counts_hbm, counts_ref), (index_hbm, index_ref), (query_hbm, query_ref)]
            + [(features_hbm.at[r], features_ref.at[r]) for r in range(recs)]
            + [(proj_hbm, proj_ref), (docs_hbm, docs_ref)]
        )
    ]
    for copy in copies:
        copy.start()
    copies[1].wait()
    group, column, tm = lax.axis_index("grp"), lax.axis_index("tm"), lax.axis_size("tm")
    layer, core = group // 2, group % 2
    row = lax.broadcasted_iota(jnp.int32, place_ref.shape, 0)
    spot = lax.broadcasted_iota(jnp.int32, place_ref.shape, 1)
    place = jnp.full(place_ref.shape, -1, jnp.int32)
    for r in range(2 * recs):
        target = index_ref[(group ^ (r // recs)) * recs + r % recs]
        of_group, rest = target // (tm * docs_dev), target % (tm * docs_dev)
        of_layer = of_group // 2
        at = (rest // docs_dev) ^ (column if by_column else 0)
        if by_layer:
            steps = of_layer ^ layer
            far = steps // 2
            at = (at * 2 + far) * docs_dev + rest % docs_dev
            chunk = steps % 2
            mine = (of_group + core) % 2 == 0
        else:
            at = (of_layer * tm + at) * docs_dev + rest % docs_dev
            chunk = 0
            mine = (of_group + core) % 2 == 0
        chunk = jnp.where(mine, chunk, -1)
        place = jnp.where((row == r) & (spot == chunk), at, place)
    place_ref[...] = place
    spot = lax.broadcasted_iota(jnp.int32, at_ref.shape, 1)
    ats = jnp.full(at_ref.shape, -1, jnp.int32)
    first = (group * tm + column) * docs_dev
    for n, block in enumerate(blocks):
        if block is not None:
            base = ((layer ^ block[0]) * 2 + (core ^ block[1])) * recs
            for r in range(recs):
                ats = jnp.where(spot == n * recs + r, index_ref[base + r] - first, ats)
    at_ref[...] = ats
    copies[0].wait()
    copies[2].wait()
    query = jnp.concatenate([query_ref[...].astype(f32), jnp.zeros((128 - heads, channels), f32)], 0).T.astype(bf16)
    start = lax.axis_index("tm") * frames
    spots = lax.broadcasted_iota(jnp.int32, (heads, frames), 1)
    scores, weights, peaks, totals, highs, lows = [], [], [], [], [], []
    for step in range(recs + 2):
        if step < recs:
            copies[3 + step].wait()
            scores.append(
                jnp.dot(features_ref[step], query, preferred_element_type=f32).T[:heads]
            )
        if 0 <= step - 1 < recs:
            r = step - 1
            valid = spots < counts_ref[r] - start
            masked = jnp.where(valid, scores[r] / math.sqrt(channels), -1e30)
            peak = jnp.max(masked, axis=1, keepdims=True).astype(bf16).astype(f32)
            weight = jnp.where(valid, jnp.exp(masked - peak), 0.0)
            peaks.append(peak)
            totals.append(jnp.sum(weight, axis=1, keepdims=True))
            weights.append(jnp.concatenate(two_terms(weight), 0))
        if 0 <= step - 2 < recs:
            r = step - 2
            both = jnp.dot(weights[r], features_ref[r], preferred_element_type=f32)
            high, low = two_terms(both[:heads] + both[heads:])
            highs.append(high)
            lows.append(low)
    peak, totals = jnp.concatenate(peaks, 0), jnp.concatenate(totals, 0)
    copies[3 + recs].wait()
    wide = jnp.dot(jnp.concatenate(highs + lows, 0), proj_ref[...], preferred_element_type=f32)
    wide = wide[:rows] + wide[rows:]
    own = lax.broadcasted_iota(jnp.int32, (rows, width), 1) // (width // heads)
    own = own == lax.broadcasted_iota(jnp.int32, (rows, width), 0) % heads
    lane = lax.broadcasted_iota(jnp.int32, (rows, 128), 1)
    lane = lane == lax.broadcasted_iota(jnp.int32, (rows, 128), 0) % heads

    def over_heads(value):
        return jnp.concatenate(
            [jnp.sum(value[r * heads : (r + 1) * heads], 0, keepdims=True) for r in range(recs)], 0
        )

    pooled = over_heads(jnp.where(own, wide, 0.0))
    pooled_high = pooled.astype(bf16).astype(f32)
    totals = over_heads(jnp.where(lane, totals, 0.0))
    totals_high = totals.astype(bf16).astype(f32)
    peaks = over_heads(jnp.where(lane, peak, 0.0))
    stats = [peaks, totals_high, totals - totals_high, jnp.zeros((recs, width - 384), f32)]
    copies[4 + recs].wait()
    out_ref[...] = jnp.concatenate(
        [pooled_high, pooled - pooled_high, jnp.concatenate(stats, 1), jnp.zeros((recs, width), f32)], 0
    ).astype(bf16)


def meet_kernel(recs, heads, doc_rows, apart, *refs):
    parts, (send_ref, both_ref) = list(refs[:-2]), refs[-2:]
    width = parts[0].shape[1]
    last = [parts.pop(), parts.pop()][::-1] if apart else []
    sums, peaks, totals = [], [], []
    for part in parts:
        pool = part[...].astype(f32)[doc_rows:]
        sums.append([pool[n : n + recs] + pool[n + recs : n + 2 * recs] for n in (0, 2 * recs)])
        peaks.append(pool[4 * recs :, :128])
        totals.append(pool[4 * recs :, 128:256] + pool[4 * recs :, 256:384])
    if apart:
        pools = [part[...].astype(f32)[part.shape[0] - 4 * recs :] for part in last]
        sums.append([pool[:recs] + pool[recs : 2 * recs] for pool in pools])
        stats = jnp.concatenate([pool[2 * recs : 3 * recs] for pool in pools], 0)
        peaks.append(stats[:, :128])
        totals.append(stats[:, 128:256] + stats[:, 256:384])
        parts.append(last[0])
    sums = [jnp.concatenate(pair, 0) for pair in sums]
    top = peaks[0]
    for peak in peaks[1:]:
        top = jnp.maximum(top, peak)
    shares = [jnp.exp(peak - top) for peak in peaks]
    whole = shares[0] * totals[0]
    for share, total in zip(shares[1:], totals[1:]):
        whole = whole + share * total
    used = lax.broadcasted_iota(jnp.int32, whole.shape, 1) < heads
    inverse = jnp.where(used, 1.0 / jnp.where(used, whole, 1.0), 0.0)
    high, low = two_terms(jnp.concatenate([share * inverse for share in shares], 0))
    spread = lax.broadcasted_iota(jnp.int32, (128, width), 1) // (width // heads)
    spread = (spread == lax.broadcasted_iota(jnp.int32, (128, width), 0)).astype(f32).astype(bf16)
    scales = jnp.dot(high, spread, preferred_element_type=f32) + jnp.dot(
        low, spread, preferred_element_type=f32
    )
    pooled = jnp.zeros((2 * recs, width), f32)
    for n, part in enumerate(sums):
        pooled = pooled + part * scales[2 * n * recs : 2 * (n + 1) * recs]
    speech = pooled * lax.rsqrt(jnp.sum(pooled * pooled, axis=1, keepdims=True) + norm_eps)
    both_ref[...] = jnp.concatenate([speech, jnp.zeros((2 * recs, width), f32)], 0).astype(bf16)
    send_ref[...] = jnp.concatenate([part[:doc_rows, :] for part in parts] + [speech.astype(bf16)], 0)


def pair_terms(logits, positive):
    logits = logit_scale * logits + logit_shift
    signed = jnp.where(positive, -logits, logits)
    losses = jnp.maximum(signed, 0.0) + jnp.log1p(jnp.exp(-jnp.abs(signed)))
    slopes = jax.nn.sigmoid(signed)
    return losses, jnp.where(positive, -slopes, slopes).astype(bf16)


def speech_terms(place_ref, chunk, speech, docs):
    logits = lax.dot_general(speech, docs, BY_ROWS, preferred_element_type=f32)
    positive = lax.broadcasted_iota(jnp.int32, logits.shape, 1) == place_ref[:, chunk : chunk + 1]
    losses, grad_b = pair_terms(logits, positive)
    grad = logit_scale * jnp.dot(grad_b, docs, preferred_element_type=f32)
    return jnp.sum(losses, axis=1, keepdims=True), grad


def first_docs_kernel(place_ref, both_ref, docs_ref, loss_ref, grad_ref):
    recs = both_ref.shape[0] // 4
    loss, grad = speech_terms(place_ref, 0, both_ref[...], docs_ref[: docs_ref.shape[0] - 2 * recs, :])
    loss_ref[...] = jnp.broadcast_to(loss, loss_ref.shape)
    grad_ref[...] = grad


def share_kernel(place_ref, both_ref, loss_ref, grad_ref, *refs):
    blocks, (loss_out, grad_out, send_ref) = refs[:-3], refs[-3:]
    recs = both_ref.shape[0] // 4
    loss, grad = loss_ref[...], grad_ref[...]
    for block in blocks:
        doc_rows = block.shape[0] - 2 * recs
        more = speech_terms(place_ref, 1, both_ref[...], block[:doc_rows, :])
        loss, grad = loss + more[0], grad + more[1]
    loss_out[...] = loss[:recs]
    grad_out[...] = grad[:recs]
    loss, grad = loss[recs : 2 * recs], grad[recs : 2 * recs]
    grad_high = grad.astype(bf16).astype(f32)
    loss_high = loss.astype(bf16).astype(f32)
    loss_low = (loss - loss_high).astype(bf16).astype(f32)
    terms = [loss_high, loss_low, loss - loss_high - loss_low]
    terms.append(jnp.zeros((recs, grad.shape[1] - 384), f32))
    send_ref[...] = jnp.concatenate(
        [grad_high, grad - grad_high, jnp.concatenate(terms, 1), jnp.zeros_like(grad)], 0
    ).astype(bf16)


def last_kernel(at_ref, docs_ref, loss_ref, grad_ref, back_ref, *refs):
    row_refs, (loss_out, speech_out, doc_out) = refs[:-3], refs[-3:]
    recs = speech_out.shape[0]
    back = back_ref[...].astype(f32)
    speech_out[...] = grad_ref[...] + back[:recs] + back[recs : 2 * recs]
    terms = back[2 * recs : 3 * recs]
    loss = loss_ref[...] + (terms[:, :128] + terms[:, 128:256] + terms[:, 256:384])
    diagonal = lax.broadcasted_iota(jnp.int32, (recs, 128), 0)
    diagonal = diagonal == lax.broadcasted_iota(jnp.int32, (recs, 128), 1)
    loss_out[...] = jnp.sum(jnp.where(diagonal, loss, 0.0), axis=0, keepdims=True)[:, :recs]
    if len(row_refs) == 1:
        rows = row_refs[0][...]
    else:
        both, near, *beyond = [ref[...].astype(f32) for ref in row_refs]
        beyond = [part[: 2 * recs] for part in beyond]
        rows = jnp.concatenate([both, near, *beyond], 0).astype(bf16)
    logits = lax.dot_general(docs_ref[...], rows, BY_ROWS, preferred_element_type=f32)
    positive = lax.broadcasted_iota(jnp.int32, logits.shape, 0) == at_ref[:1, : logits.shape[1]]
    _, grad_b = pair_terms(logits, positive)
    doc_out[...] = logit_scale * jnp.dot(grad_b, rows, preferred_element_type=f32)


def swap_pairs(count, stride, steps):
    return [(source, source ^ (steps * stride)) for source in range(count)]


def is_direct(extent):
    return extent <= direct_limit and extent & (extent - 1) == 0


def to_other_core(value):
    return lax.ppermute(value, "grp", swap_pairs(lax.axis_size("grp"), 1, 1))


def across(value, layer_steps, column_steps, core_steps=0):
    columns = lax.axis_size("tm")
    steps = (2 * layer_steps + core_steps) * columns + column_steps
    return lax.ppermute(value, ("grp", "tm"), swap_pairs(lax.axis_size("grp") * columns, 1, steps))


def body(features, frame_counts, pool_query, w_proj, doc_embed, doc_index):
    recs, frames, channels = features.shape
    heads, width = pool_query.shape[0], w_proj.shape[1]
    docs_dev = doc_embed.shape[0]
    groups, columns = lax.axis_size("grp"), lax.axis_size("tm")
    layers = groups // 2
    direct = layers == 4
    order = (2, 3) if direct else ()

    def shape(rows, lanes, kind=f32):
        return jax.ShapeDtypeStruct((rows, lanes), kind)

    blocks = []
    if direct:
        blocks = [(0, 0), (0, 1), None, None, (1, 0), (1, 1)]
        blocks += [(steps, flip) for steps in order for flip in (1, 0)]
        far = across(doc_embed, 2, 0)
    docs, pools, place, at = pl.pallas_call(
        lambda *refs: pool_kernel((docs_dev, is_direct(columns), direct), blocks, *refs),
        out_shape=(
            shape(docs_dev, width, bf16),
            shape(4 * recs, width, bf16),
            shape(4 * recs, 128, jnp.int32),
            shape(8, 128, jnp.int32),
        ),
        in_specs=[pl.BlockSpec(memory_space=pltpu.HBM)] * 6,
        out_specs=(VMEM,) * 4,
        scratch_shapes=[
            pltpu.SMEM(frame_counts.shape, jnp.int32),
            pltpu.SMEM(doc_index.shape, jnp.int32),
            pltpu.VMEM(pool_query.shape, bf16),
            pltpu.VMEM(features.shape, bf16),
            pltpu.VMEM(w_proj.shape, bf16),
            pltpu.SemaphoreType.DMA((recs + 5,)),
        ],
        compiler_params=pltpu.CompilerParams(vmem_limit_bytes=12 * 2**20),
        name="pool",
    )(
        *[
            pltpu.with_memory_space_constraint(operand, pltpu.HBM)
            for operand in (frame_counts, doc_index, pool_query, features, w_proj, doc_embed)
        ]
    )
    other = to_other_core(pools)
    docs = [docs, *([far] if direct else [])]
    payload = [pools[: 2 * recs], other[: 2 * recs], pools[2 * recs : 3 * recs], other[2 * recs : 3 * recs]]
    payload = jnp.concatenate([*docs, *payload])
    parts = [payload]
    doc_rows = columns * (payload.shape[0] - 6 * recs)
    if is_direct(columns):
        parts += [across(payload, 0, steps) for steps in range(1, columns - 1)]
        parts.append(across(jnp.concatenate([*docs, pools]), 0, columns - 1))
        parts.append(to_other_core(parts[-1][doc_rows // columns :]))
    else:
        parts = list(lax.all_gather(payload, "tm"))
    own, both = in_vmem(
        lambda *refs: meet_kernel(recs, heads, doc_rows // columns, is_direct(columns), *refs),
        (shape(doc_rows + 2 * recs, width, bf16), shape(4 * recs, width, bf16)),
        8,
        "meet",
    )(*parts)

    docs, near = own, []
    if direct:
        near = [across(own, 1, 0)]
        beyond = [across(both, steps, 0, 1) for steps in order]
    else:
        same_core = [[2 * n + core for n in range(layers)] for core in range(2)]
        docs = lax.all_gather(own[:doc_rows], "grp", axis_index_groups=same_core, tiled=True)
        docs = jnp.concatenate([docs, own[doc_rows:]])
    loss, grad = in_vmem(
        first_docs_kernel,
        (shape(4 * recs, 128), shape(4 * recs, width)),
        8 + docs.shape[0] // 128,
        "first_docs",
    )(place, both, docs)
    loss, grad, send = in_vmem(
        share_kernel,
        (shape(recs, 128), shape(recs, width), shape(4 * recs, width, bf16)),
        8,
        "share",
    )(place, both, loss, grad, *near)
    back = to_other_core(send)
    if direct:
        rows = (both, near[0][doc_rows:], *beyond)
    else:
        rows = (lax.all_gather(both[:recs], "grp", tiled=True),)
        at = doc_index[None, :] - (lax.axis_index("grp") * columns + lax.axis_index("tm")) * docs_dev
    loss, speech_grad, doc_grad = in_vmem(
        last_kernel,
        (shape(1, recs), shape(recs, width), shape(docs_dev, width)),
        8,
        "last",
    )(at, doc_embed, loss, grad, back, *rows)
    return (loss[0], speech_grad, doc_grad)


def solution(mesh):
    placed = (P("grp", "tm", None), P("grp"), P(), P(), P(("grp", "tm"), None), P())
    return jax.shard_map(
        body,
        mesh=mesh,
        in_specs=placed,
        out_specs=(P("grp"), P("grp", None), P(("grp", "tm"), None)),
        check_vma=False,
    )
```

```python
import math

import jax
import jax.numpy as jnp
from jax import lax
from jax.experimental import pallas as pl
from jax.experimental.pallas import tpu as pltpu
from jax.sharding import PartitionSpec as P

logit_scale = 10.0
logit_shift = -8.0
norm_eps = 1e-06
direct_limit = 8
bf16 = jnp.bfloat16
f32 = jnp.float32
BY_ROWS = (((1,), (1,)), ((), ()))
VMEM = pl.BlockSpec(memory_space=pltpu.VMEM)


def in_vmem(kernel, outs, limit_mib, name):
    def call(*operands):
        return pl.pallas_call(
            kernel,
            out_shape=outs,
            in_specs=[VMEM] * len(operands),
            out_specs=jax.tree.map(lambda _: VMEM, outs),
            compiler_params=pltpu.CompilerParams(vmem_limit_bytes=limit_mib * 2**20),
            name=name,
        )(*operands)

    return call


def two_terms(value):
    high = value.astype(bf16)
    return high, (value - high.astype(f32)).astype(bf16)


def pool_kernel(
    scheme,
    blocks,
    counts_hbm,
    index_hbm,
    query_hbm,
    features_hbm,
    proj_hbm,
    docs_hbm,
    docs_ref,
    out_ref,
    place_ref,
    at_ref,
    counts_ref,
    index_ref,
    query_ref,
    features_ref,
    proj_ref,
    sems,
):
    recs, frames, channels = features_ref.shape
    heads = query_ref.shape[0]
    width = proj_ref.shape[1]
    rows = recs * heads
    docs_dev, by_column, by_layer = scheme
    copies = [
        pltpu.make_async_copy(source, target, sems.at[n])
        for n, (source, target) in enumerate(
            [(counts_hbm, counts_ref), (index_hbm, index_ref), (query_hbm, query_ref)]
            + [(features_hbm.at[r], features_ref.at[r]) for r in range(recs)]
            + [(proj_hbm, proj_ref), (docs_hbm, docs_ref)]
        )
    ]
    for copy in copies:
        copy.start()
    copies[1].wait()
    group, column, tm = lax.axis_index("grp"), lax.axis_index("tm"), lax.axis_size("tm")
    layer, core = group // 2, group % 2
    row = lax.broadcasted_iota(jnp.int32, place_ref.shape, 0)
    spot = lax.broadcasted_iota(jnp.int32, place_ref.shape, 1)
    place = jnp.full(place_ref.shape, -1, jnp.int32)
    for r in range(2 * recs):
        target = index_ref[(group ^ (r // recs)) * recs + r % recs]
        of_group, rest = target // (tm * docs_dev), target % (tm * docs_dev)
        of_layer = of_group // 2
        at = (rest // docs_dev) ^ (column if by_column else 0)
        crossed = of_group + core
        if by_column:
            crossed = crossed + jnp.where(at == tm - 1, 1, 0)
        if by_layer:
            steps = of_layer ^ layer
            far = steps // 2
            at = (at * 2 + far) * docs_dev + rest % docs_dev
            chunk = steps % 2
            crossed = crossed + far
        else:
            at = (of_layer * tm + at) * docs_dev + rest % docs_dev
            chunk = 0
        mine = crossed % 2 == 0
        chunk = jnp.where(mine, chunk, -1)
        place = jnp.where((row == r) & (spot == chunk), at, place)
    place_ref[...] = place
    spot = lax.broadcasted_iota(jnp.int32, at_ref.shape, 1)
    ats = jnp.full(at_ref.shape, -1, jnp.int32)
    first = (group * tm + column) * docs_dev
    for n, block in enumerate(blocks):
        if block is not None:
            base = ((layer ^ block[0]) * 2 + (core ^ block[1])) * recs
            for r in range(recs):
                ats = jnp.where(spot == n * recs + r, index_ref[base + r] - first, ats)
    at_ref[...] = ats
    copies[0].wait()
    copies[2].wait()
    query = jnp.concatenate([query_ref[...].astype(f32), jnp.zeros((128 - heads, channels), f32)], 0).T.astype(bf16)
    start = lax.axis_index("tm") * frames
    spots = lax.broadcasted_iota(jnp.int32, (heads, frames), 1)
    scores, weights, peaks, totals, highs, lows = [], [], [], [], [], []
    for step in range(recs + 2):
        if step < recs:
            copies[3 + step].wait()
            scores.append(
                jnp.dot(features_ref[step], query, preferred_element_type=f32).T[:heads]
            )
        if 0 <= step - 1 < recs:
            r = step - 1
            valid = spots < counts_ref[r] - start
            masked = jnp.where(valid, scores[r] / math.sqrt(channels), -1e30)
            peak = jnp.max(masked, axis=1, keepdims=True).astype(bf16).astype(f32)
            weight = jnp.where(valid, jnp.exp(masked - peak), 0.0)
            peaks.append(peak)
            totals.append(jnp.sum(weight, axis=1, keepdims=True))
            weights.append(jnp.concatenate(two_terms(weight), 0))
        if 0 <= step - 2 < recs:
            r = step - 2
            both = jnp.dot(weights[r], features_ref[r], preferred_element_type=f32)
            high, low = two_terms(both[:heads] + both[heads:])
            highs.append(high)
            lows.append(low)
    peak, totals = jnp.concatenate(peaks, 0), jnp.concatenate(totals, 0)
    copies[3 + recs].wait()
    wide = jnp.dot(jnp.concatenate(highs + lows, 0), proj_ref[...], preferred_element_type=f32)
    wide = wide[:rows] + wide[rows:]
    own = lax.broadcasted_iota(jnp.int32, (rows, width), 1) // (width // heads)
    own = own == lax.broadcasted_iota(jnp.int32, (rows, width), 0) % heads
    lane = lax.broadcasted_iota(jnp.int32, (rows, 128), 1)
    lane = lane == lax.broadcasted_iota(jnp.int32, (rows, 128), 0) % heads

    def over_heads(value):
        return jnp.concatenate(
            [jnp.sum(value[r * heads : (r + 1) * heads], 0, keepdims=True) for r in range(recs)], 0
        )

    pooled = over_heads(jnp.where(own, wide, 0.0))
    pooled_high = pooled.astype(bf16).astype(f32)
    totals = over_heads(jnp.where(lane, totals, 0.0))
    totals_high = totals.astype(bf16).astype(f32)
    peaks = over_heads(jnp.where(lane, peak, 0.0))
    stats = [peaks, totals_high, totals - totals_high, jnp.zeros((recs, width - 384), f32)]
    copies[4 + recs].wait()
    out_ref[...] = jnp.concatenate(
        [pooled_high, pooled - pooled_high, jnp.concatenate(stats, 1), jnp.zeros((recs, width), f32)], 0
    ).astype(bf16)


def meet_kernel(recs, heads, doc_rows, apart, *refs):
    parts, (send_ref, both_ref) = list(refs[:-2]), refs[-2:]
    width = parts[0].shape[1]
    last = [parts.pop(), parts.pop()][::-1] if apart else []
    sums, peaks, totals = [], [], []
    for part in parts:
        pool = part[...].astype(f32)[doc_rows:]
        sums.append([pool[n : n + recs] + pool[n + recs : n + 2 * recs] for n in (0, 2 * recs)])
        peaks.append(pool[4 * recs :, :128])
        totals.append(pool[4 * recs :, 128:256] + pool[4 * recs :, 256:384])
    if apart:
        pools = [part[...].astype(f32)[part.shape[0] - 4 * recs :] for part in last[::-1]]
        sums.append([pool[:recs] + pool[recs : 2 * recs] for pool in pools])
        stats = jnp.concatenate([pool[2 * recs : 3 * recs] for pool in pools], 0)
        peaks.append(stats[:, :128])
        totals.append(stats[:, 128:256] + stats[:, 256:384])
        parts.append(last[0])
    sums = [jnp.concatenate(pair, 0) for pair in sums]
    top = peaks[0]
    for peak in peaks[1:]:
        top = jnp.maximum(top, peak)
    shares = [jnp.exp(peak - top) for peak in peaks]
    whole = shares[0] * totals[0]
    for share, total in zip(shares[1:], totals[1:]):
        whole = whole + share * total
    used = lax.broadcasted_iota(jnp.int32, whole.shape, 1) < heads
    inverse = jnp.where(used, 1.0 / jnp.where(used, whole, 1.0), 0.0)
    high, low = two_terms(jnp.concatenate([share * inverse for share in shares], 0))
    spread = lax.broadcasted_iota(jnp.int32, (128, width), 1) // (width // heads)
    spread = (spread == lax.broadcasted_iota(jnp.int32, (128, width), 0)).astype(f32).astype(bf16)
    scales = jnp.dot(high, spread, preferred_element_type=f32) + jnp.dot(
        low, spread, preferred_element_type=f32
    )
    pooled = jnp.zeros((2 * recs, width), f32)
    for n, part in enumerate(sums):
        pooled = pooled + part * scales[2 * n * recs : 2 * (n + 1) * recs]
    speech = pooled * lax.rsqrt(jnp.sum(pooled * pooled, axis=1, keepdims=True) + norm_eps)
    both_ref[...] = jnp.concatenate([speech, jnp.zeros((2 * recs, width), f32)], 0).astype(bf16)
    send_ref[...] = jnp.concatenate([part[:doc_rows, :] for part in parts] + [speech.astype(bf16)], 0)


def pair_terms(logits, positive):
    logits = logit_scale * logits + logit_shift
    signed = jnp.where(positive, -logits, logits)
    losses = jnp.maximum(signed, 0.0) + jnp.log1p(jnp.exp(-jnp.abs(signed)))
    slopes = jax.nn.sigmoid(signed)
    return losses, jnp.where(positive, -slopes, slopes).astype(bf16)


def speech_terms(place_ref, chunk, speech, docs):
    logits = lax.dot_general(speech, docs, BY_ROWS, preferred_element_type=f32)
    positive = lax.broadcasted_iota(jnp.int32, logits.shape, 1) == place_ref[:, chunk : chunk + 1]
    losses, grad_b = pair_terms(logits, positive)
    grad = logit_scale * jnp.dot(grad_b, docs, preferred_element_type=f32)
    return jnp.sum(losses, axis=1, keepdims=True), grad


def first_docs_kernel(place_ref, both_ref, docs_ref, loss_ref, grad_ref):
    recs = both_ref.shape[0] // 4
    loss, grad = speech_terms(place_ref, 0, both_ref[...], docs_ref[: docs_ref.shape[0] - 2 * recs, :])
    loss_ref[...] = jnp.broadcast_to(loss, loss_ref.shape)
    grad_ref[...] = grad


def share_kernel(place_ref, both_ref, loss_ref, grad_ref, *refs):
    blocks, (loss_out, grad_out, send_ref) = refs[:-3], refs[-3:]
    recs = both_ref.shape[0] // 4
    loss, grad = loss_ref[...], grad_ref[...]
    for block in blocks:
        doc_rows = block.shape[0] - 2 * recs
        more = speech_terms(place_ref, 1, both_ref[...], block[:doc_rows, :])
        loss, grad = loss + more[0], grad + more[1]
    loss_out[...] = loss[:recs]
    grad_out[...] = grad[:recs]
    loss, grad = loss[recs : 2 * recs], grad[recs : 2 * recs]
    grad_high = grad.astype(bf16).astype(f32)
    loss_high = loss.astype(bf16).astype(f32)
    loss_low = (loss - loss_high).astype(bf16).astype(f32)
    terms = [loss_high, loss_low, loss - loss_high - loss_low]
    terms.append(jnp.zeros((recs, grad.shape[1] - 384), f32))
    send_ref[...] = jnp.concatenate(
        [grad_high, grad - grad_high, jnp.concatenate(terms, 1), jnp.zeros_like(grad)], 0
    ).astype(bf16)


def last_kernel(at_ref, docs_ref, loss_ref, grad_ref, back_ref, *refs):
    row_refs, (loss_out, speech_out, doc_out) = refs[:-3], refs[-3:]
    recs = speech_out.shape[0]
    back = back_ref[...].astype(f32)
    speech_out[...] = grad_ref[...] + back[:recs] + back[recs : 2 * recs]
    terms = back[2 * recs : 3 * recs]
    loss = loss_ref[...] + (terms[:, :128] + terms[:, 128:256] + terms[:, 256:384])
    diagonal = lax.broadcasted_iota(jnp.int32, (recs, 128), 0)
    diagonal = diagonal == lax.broadcasted_iota(jnp.int32, (recs, 128), 1)
    loss_out[...] = jnp.sum(jnp.where(diagonal, loss, 0.0), axis=0, keepdims=True)[:, :recs]
    if len(row_refs) == 1:
        rows = row_refs[0][...]
    else:
        both, near, *beyond = [ref[...].astype(f32) for ref in row_refs]
        beyond = [part[: 2 * recs] for part in beyond]
        rows = jnp.concatenate([both, near, *beyond], 0).astype(bf16)
    logits = lax.dot_general(docs_ref[...], rows, BY_ROWS, preferred_element_type=f32)
    positive = lax.broadcasted_iota(jnp.int32, logits.shape, 0) == at_ref[:1, : logits.shape[1]]
    _, grad_b = pair_terms(logits, positive)
    doc_out[...] = logit_scale * jnp.dot(grad_b, rows, preferred_element_type=f32)


def swap_pairs(count, stride, steps):
    return [(source, source ^ (steps * stride)) for source in range(count)]


def is_direct(extent):
    return extent <= direct_limit and extent & (extent - 1) == 0


def to_other_core(value):
    return lax.ppermute(value, "grp", swap_pairs(lax.axis_size("grp"), 1, 1))


def across(value, layer_steps, column_steps, core_steps=0):
    columns = lax.axis_size("tm")
    steps = (2 * layer_steps + core_steps) * columns + column_steps
    return lax.ppermute(value, ("grp", "tm"), swap_pairs(lax.axis_size("grp") * columns, 1, steps))


def body(features, frame_counts, pool_query, w_proj, doc_embed, doc_index):
    recs, frames, channels = features.shape
    heads, width = pool_query.shape[0], w_proj.shape[1]
    docs_dev = doc_embed.shape[0]
    groups, columns = lax.axis_size("grp"), lax.axis_size("tm")
    layers = groups // 2
    direct = layers == 4
    order = (2, 3) if direct else ()

    def shape(rows, lanes, kind=f32):
        return jax.ShapeDtypeStruct((rows, lanes), kind)

    blocks = []
    if direct:
        blocks = [(0, 0), (0, 1), None, None, (1, 0), (1, 1)]
        blocks += [(steps, flip) for steps in order for flip in (1, 0)]
        far = across(doc_embed, 2, 0, 1)
    docs, pools, place, at = pl.pallas_call(
        lambda *refs: pool_kernel((docs_dev, is_direct(columns), direct), blocks, *refs),
        out_shape=(
            shape(docs_dev, width, bf16),
            shape(4 * recs, width, bf16),
            shape(4 * recs, 128, jnp.int32),
            shape(8, 128, jnp.int32),
        ),
        in_specs=[pl.BlockSpec(memory_space=pltpu.HBM)] * 6,
        out_specs=(VMEM,) * 4,
        scratch_shapes=[
            pltpu.SMEM(frame_counts.shape, jnp.int32),
            pltpu.SMEM(doc_index.shape, jnp.int32),
            pltpu.VMEM(pool_query.shape, bf16),
            pltpu.VMEM(features.shape, bf16),
            pltpu.VMEM(w_proj.shape, bf16),
            pltpu.SemaphoreType.DMA((recs + 5,)),
        ],
        compiler_params=pltpu.CompilerParams(vmem_limit_bytes=12 * 2**20),
        name="pool",
    )(
        *[
            pltpu.with_memory_space_constraint(operand, pltpu.HBM)
            for operand in (frame_counts, doc_index, pool_query, features, w_proj, doc_embed)
        ]
    )
    other = to_other_core(pools)
    docs = [docs, *([far] if direct else [])]
    payload = [pools[: 2 * recs], other[: 2 * recs], pools[2 * recs : 3 * recs], other[2 * recs : 3 * recs]]
    payload = jnp.concatenate([*docs, *payload])
    parts = [payload]
    doc_rows = columns * (payload.shape[0] - 6 * recs)
    if is_direct(columns):
        parts += [across(payload, 0, steps) for steps in range(1, columns - 1)]
        parts.append(across(jnp.concatenate([*docs, pools]), 0, columns - 1, 1))
        parts.append(to_other_core(parts[-1][doc_rows // columns :]))
    else:
        parts = list(lax.all_gather(payload, "tm"))
    own, both = in_vmem(
        lambda *refs: meet_kernel(recs, heads, doc_rows // columns, is_direct(columns), *refs),
        (shape(doc_rows + 2 * recs, width, bf16), shape(4 * recs, width, bf16)),
        8,
        "meet",
    )(*parts)

    docs, near = own, []
    if direct:
        near = [across(own, 1, 0)]
        beyond = [across(both, steps, 0, 1) for steps in order]
    else:
        same_core = [[2 * n + core for n in range(layers)] for core in range(2)]
        docs = lax.all_gather(own[:doc_rows], "grp", axis_index_groups=same_core, tiled=True)
        docs = jnp.concatenate([docs, own[doc_rows:]])
    loss, grad = in_vmem(
        first_docs_kernel,
        (shape(4 * recs, 128), shape(4 * recs, width)),
        8 + docs.shape[0] // 128,
        "first_docs",
    )(place, both, docs)
    loss, grad, send = in_vmem(
        share_kernel,
        (shape(recs, 128), shape(recs, width), shape(4 * recs, width, bf16)),
        8,
        "share",
    )(place, both, loss, grad, *near)
    back = to_other_core(send)
    if direct:
        rows = (both, near[0][doc_rows:], *beyond)
    else:
        rows = (lax.all_gather(both[:recs], "grp", tiled=True),)
        at = doc_index[None, :] - (lax.axis_index("grp") * columns + lax.axis_index("tm")) * docs_dev
    loss, speech_grad, doc_grad = in_vmem(
        last_kernel,
        (shape(1, recs), shape(recs, width), shape(docs_dev, width)),
        8,
        "last",
    )(at, doc_embed, loss, grad, back, *rows)
    return (loss[0], speech_grad, doc_grad)


def solution(mesh):
    placed = (P("grp", "tm", None), P("grp"), P(), P(), P(("grp", "tm"), None), P())
    return jax.shard_map(
        body,
        mesh=mesh,
        in_specs=placed,
        out_specs=(P("grp"), P("grp", None), P(("grp", "tm"), None)),
        check_vma=False,
    )
```

```python
import math

import jax
import jax.numpy as jnp
from jax import lax
from jax.experimental import pallas as pl
from jax.experimental.pallas import tpu as pltpu
from jax.sharding import PartitionSpec as P

logit_scale = 10.0
logit_shift = -8.0
norm_eps = 1e-06
direct_limit = 8
bf16 = jnp.bfloat16
f32 = jnp.float32
BY_ROWS = (((1,), (1,)), ((), ()))
VMEM = pl.BlockSpec(memory_space=pltpu.VMEM)


def in_vmem(kernel, outs, limit_mib, name):
    def call(*operands):
        return pl.pallas_call(
            kernel,
            out_shape=outs,
            in_specs=[VMEM] * len(operands),
            out_specs=jax.tree.map(lambda _: VMEM, outs),
            compiler_params=pltpu.CompilerParams(vmem_limit_bytes=limit_mib * 2**20),
            name=name,
        )(*operands)

    return call


def two_terms(value):
    high = value.astype(bf16)
    return high, (value - high.astype(f32)).astype(bf16)


def pool_kernel(
    scheme,
    blocks,
    counts_hbm,
    index_hbm,
    query_hbm,
    features_hbm,
    proj_hbm,
    docs_hbm,
    docs_ref,
    out_ref,
    place_ref,
    at_ref,
    counts_ref,
    index_ref,
    query_ref,
    features_ref,
    proj_ref,
    sems,
):
    recs, frames, channels = features_ref.shape
    heads = query_ref.shape[0]
    width = proj_ref.shape[1]
    rows = recs * heads
    docs_dev, by_column, by_layer = scheme
    copies = [
        pltpu.make_async_copy(source, target, sems.at[n])
        for n, (source, target) in enumerate(
            [(counts_hbm, counts_ref), (index_hbm, index_ref), (query_hbm, query_ref)]
            + [(features_hbm.at[r], features_ref.at[r]) for r in range(recs)]
            + [(proj_hbm, proj_ref), (docs_hbm, docs_ref)]
        )
    ]
    for copy in copies:
        copy.start()
    copies[1].wait()
    group, column, tm = lax.axis_index("grp"), lax.axis_index("tm"), lax.axis_size("tm")
    layer, core = group // 2, group % 2
    row = lax.broadcasted_iota(jnp.int32, place_ref.shape, 0)
    spot = lax.broadcasted_iota(jnp.int32, place_ref.shape, 1)
    place = jnp.full(place_ref.shape, -1, jnp.int32)
    for r in range(2 * recs):
        target = index_ref[(group ^ (r // recs)) * recs + r % recs]
        of_group, rest = target // (tm * docs_dev), target % (tm * docs_dev)
        of_layer = of_group // 2
        at = (rest // docs_dev) ^ (column if by_column else 0)
        crossed = of_group + core
        if by_column:
            crossed = crossed + jnp.where(at == tm - 1, 1, 0)
        if by_layer:
            steps = of_layer ^ layer
            far = steps // 2
            at = (at * 2 + far) * docs_dev + rest % docs_dev
            chunk = steps % 2
            crossed = crossed + far
        else:
            at = (of_layer * tm + at) * docs_dev + rest % docs_dev
            chunk = 0
        mine = crossed % 2 == 0
        chunk = jnp.where(mine, chunk, -1)
        place = jnp.where((row == r) & (spot == chunk), at, place)
    place_ref[...] = place
    spot = lax.broadcasted_iota(jnp.int32, at_ref.shape, 1)
    ats = jnp.full(at_ref.shape, -1, jnp.int32)
    first = (group * tm + column) * docs_dev
    for n, block in enumerate(blocks):
        if block is not None:
            base = ((layer ^ block[0]) * 2 + (core ^ block[1])) * recs
            for r in range(recs):
                ats = jnp.where(spot == n * recs + r, index_ref[base + r] - first, ats)
    at_ref[...] = ats
    copies[0].wait()
    copies[2].wait()
    query = jnp.concatenate([query_ref[...].astype(f32), jnp.zeros((128 - heads, channels), f32)], 0).T.astype(bf16)
    start = lax.axis_index("tm") * frames
    spots = lax.broadcasted_iota(jnp.int32, (heads, frames), 1)
    scores, weights, peaks, totals, highs, lows = [], [], [], [], [], []
    for step in range(recs + 2):
        if step < recs:
            copies[3 + step].wait()
            scores.append(
                jnp.dot(features_ref[step], query, preferred_element_type=f32).T[:heads]
            )
        if 0 <= step - 1 < recs:
            r = step - 1
            valid = spots < counts_ref[r] - start
            masked = jnp.where(valid, scores[r] / math.sqrt(channels), -1e30)
            peak = jnp.max(masked, axis=1, keepdims=True).astype(bf16).astype(f32)
            weight = jnp.where(valid, jnp.exp(masked - peak), 0.0)
            peaks.append(peak)
            totals.append(jnp.sum(weight, axis=1, keepdims=True))
            weights.append(jnp.concatenate(two_terms(weight), 0))
        if 0 <= step - 2 < recs:
            r = step - 2
            both = jnp.dot(weights[r], features_ref[r], preferred_element_type=f32)
            high, low = two_terms(both[:heads] + both[heads:])
            highs.append(high)
            lows.append(low)
    peak, totals = jnp.concatenate(peaks, 0), jnp.concatenate(totals, 0)
    copies[3 + recs].wait()
    wide = jnp.dot(jnp.concatenate(highs + lows, 0), proj_ref[...], preferred_element_type=f32)
    wide = wide[:rows] + wide[rows:]
    own = lax.broadcasted_iota(jnp.int32, (rows, width), 1) // (width // heads)
    own = own == lax.broadcasted_iota(jnp.int32, (rows, width), 0) % heads
    lane = lax.broadcasted_iota(jnp.int32, (rows, 128), 1)
    lane = lane == lax.broadcasted_iota(jnp.int32, (rows, 128), 0) % heads

    def over_heads(value):
        return jnp.concatenate(
            [jnp.sum(value[r * heads : (r + 1) * heads], 0, keepdims=True) for r in range(recs)], 0
        )

    pooled = over_heads(jnp.where(own, wide, 0.0))
    pooled_high = pooled.astype(bf16).astype(f32)
    totals = over_heads(jnp.where(lane, totals, 0.0))
    totals_high = totals.astype(bf16).astype(f32)
    peaks = over_heads(jnp.where(lane, peak, 0.0))
    stats = [peaks, totals_high, totals - totals_high, jnp.zeros((recs, width - 384), f32)]
    copies[4 + recs].wait()
    out_ref[...] = jnp.concatenate(
        [pooled_high, pooled - pooled_high, jnp.concatenate(stats, 1), jnp.zeros((recs, width), f32)], 0
    ).astype(bf16)


def meet_kernel(recs, heads, doc_rows, apart, *refs):
    parts, (send_ref, both_ref) = list(refs[:-2]), refs[-2:]
    width = parts[0].shape[1]
    last = [parts.pop(), parts.pop()][::-1] if apart else []
    sums, peaks, totals = [], [], []
    for part in parts:
        pool = part[...].astype(f32)[doc_rows:]
        sums.append([pool[n : n + recs] + pool[n + recs : n + 2 * recs] for n in (0, 2 * recs)])
        peaks.append(pool[4 * recs :, :128])
        totals.append(pool[4 * recs :, 128:256] + pool[4 * recs :, 256:384])
    if apart:
        pools = [part[...].astype(f32)[part.shape[0] - 4 * recs :] for part in last[::-1]]
        sums.append([pool[:recs] + pool[recs : 2 * recs] for pool in pools])
        stats = jnp.concatenate([pool[2 * recs : 3 * recs] for pool in pools], 0)
        peaks.append(stats[:, :128])
        totals.append(stats[:, 128:256] + stats[:, 256:384])
        parts.append(last[0])
    sums = [jnp.concatenate(pair, 0) for pair in sums]
    top = peaks[0]
    for peak in peaks[1:]:
        top = jnp.maximum(top, peak)
    shares = [jnp.exp(peak - top) for peak in peaks]
    whole = shares[0] * totals[0]
    for share, total in zip(shares[1:], totals[1:]):
        whole = whole + share * total
    used = lax.broadcasted_iota(jnp.int32, whole.shape, 1) < heads
    inverse = jnp.where(used, 1.0 / jnp.where(used, whole, 1.0), 0.0)
    high, low = two_terms(jnp.concatenate([share * inverse for share in shares], 0))
    spread = lax.broadcasted_iota(jnp.int32, (16, width), 1) // (width // heads)
    spread = (spread == lax.broadcasted_iota(jnp.int32, (16, width), 0)).astype(f32).astype(bf16)
    scales = jnp.dot(jnp.concatenate([high, low], 0)[:, :16], spread, preferred_element_type=f32)
    scales = scales[: high.shape[0]] + scales[high.shape[0] :]
    pooled = jnp.zeros((2 * recs, width), f32)
    for n, part in enumerate(sums):
        pooled = pooled + part * scales[2 * n * recs : 2 * (n + 1) * recs]
    speech = pooled * lax.rsqrt(jnp.sum(pooled * pooled, axis=1, keepdims=True) + norm_eps)
    both_ref[...] = jnp.concatenate([speech, jnp.zeros((2 * recs, width), f32)], 0).astype(bf16)
    send_ref[...] = jnp.concatenate([part[:doc_rows, :] for part in parts] + [speech.astype(bf16)], 0)


def pair_terms(logits, positive):
    logits = logit_scale * logits + logit_shift
    signed = jnp.where(positive, -logits, logits)
    losses = jnp.maximum(signed, 0.0) + jnp.log1p(jnp.exp(-jnp.abs(signed)))
    slopes = jax.nn.sigmoid(signed)
    return losses, jnp.where(positive, -slopes, slopes).astype(bf16)


def speech_terms(place_ref, chunk, speech, docs):
    logits = lax.dot_general(speech, docs, BY_ROWS, preferred_element_type=f32)
    positive = lax.broadcasted_iota(jnp.int32, logits.shape, 1) == place_ref[:, chunk : chunk + 1]
    losses, grad_b = pair_terms(logits, positive)
    grad = logit_scale * jnp.dot(grad_b, docs, preferred_element_type=f32)
    return jnp.sum(losses, axis=1, keepdims=True), grad


def first_docs_kernel(place_ref, both_ref, docs_ref, loss_ref, grad_ref):
    recs = both_ref.shape[0] // 4
    loss, grad = speech_terms(place_ref, 0, both_ref[...], docs_ref[: docs_ref.shape[0] - 2 * recs, :])
    loss_ref[...] = jnp.broadcast_to(loss, loss_ref.shape)
    grad_ref[...] = grad


def share_kernel(place_ref, both_ref, loss_ref, grad_ref, *refs):
    blocks, (loss_out, grad_out, send_ref) = refs[:-3], refs[-3:]
    recs = both_ref.shape[0] // 4
    loss, grad = loss_ref[...], grad_ref[...]
    for block in blocks:
        doc_rows = block.shape[0] - 2 * recs
        more = speech_terms(place_ref, 1, both_ref[...], block[:doc_rows, :])
        loss, grad = loss + more[0], grad + more[1]
    loss_out[...] = loss[:recs]
    grad_out[...] = grad[:recs]
    loss, grad = loss[recs : 2 * recs], grad[recs : 2 * recs]
    grad_high = grad.astype(bf16).astype(f32)
    loss_high = loss.astype(bf16).astype(f32)
    loss_low = (loss - loss_high).astype(bf16).astype(f32)
    terms = [loss_high, loss_low, loss - loss_high - loss_low]
    terms.append(jnp.zeros((recs, grad.shape[1] - 384), f32))
    send_ref[...] = jnp.concatenate(
        [grad_high, grad - grad_high, jnp.concatenate(terms, 1), jnp.zeros_like(grad)], 0
    ).astype(bf16)


def last_kernel(at_ref, docs_ref, loss_ref, grad_ref, back_ref, *refs):
    row_refs, (loss_out, speech_out, doc_out) = refs[:-3], refs[-3:]
    recs = speech_out.shape[0]
    back = back_ref[...].astype(f32)
    speech_out[...] = grad_ref[...] + back[:recs] + back[recs : 2 * recs]
    terms = back[2 * recs : 3 * recs]
    loss = loss_ref[...] + (terms[:, :128] + terms[:, 128:256] + terms[:, 256:384])
    diagonal = lax.broadcasted_iota(jnp.int32, (recs, 128), 0)
    diagonal = diagonal == lax.broadcasted_iota(jnp.int32, (recs, 128), 1)
    loss_out[...] = jnp.sum(jnp.where(diagonal, loss, 0.0), axis=0, keepdims=True)[:, :recs]
    if len(row_refs) == 1:
        rows = row_refs[0][...]
    else:
        both, near, *beyond = [ref[...].astype(f32) for ref in row_refs]
        beyond = [part[: 2 * recs] for part in beyond]
        rows = jnp.concatenate([both, near, *beyond], 0).astype(bf16)
    logits = lax.dot_general(docs_ref[...], rows, BY_ROWS, preferred_element_type=f32)
    positive = lax.broadcasted_iota(jnp.int32, logits.shape, 0) == at_ref[:1, : logits.shape[1]]
    _, grad_b = pair_terms(logits, positive)
    doc_out[...] = logit_scale * jnp.dot(grad_b, rows, preferred_element_type=f32)


def swap_pairs(count, stride, steps):
    return [(source, source ^ (steps * stride)) for source in range(count)]


def is_direct(extent):
    return extent <= direct_limit and extent & (extent - 1) == 0


def to_other_core(value):
    return lax.ppermute(value, "grp", swap_pairs(lax.axis_size("grp"), 1, 1))


def across(value, layer_steps, column_steps, core_steps=0):
    columns = lax.axis_size("tm")
    steps = (2 * layer_steps + core_steps) * columns + column_steps
    return lax.ppermute(value, ("grp", "tm"), swap_pairs(lax.axis_size("grp") * columns, 1, steps))


def body(features, frame_counts, pool_query, w_proj, doc_embed, doc_index):
    recs, frames, channels = features.shape
    heads, width = pool_query.shape[0], w_proj.shape[1]
    docs_dev = doc_embed.shape[0]
    groups, columns = lax.axis_size("grp"), lax.axis_size("tm")
    layers = groups // 2
    direct = layers == 4
    order = (2, 3) if direct else ()

    def shape(rows, lanes, kind=f32):
        return jax.ShapeDtypeStruct((rows, lanes), kind)

    blocks = []
    if direct:
        blocks = [(0, 0), (0, 1), None, None, (1, 0), (1, 1)]
        blocks += [(steps, flip) for steps in order for flip in (1, 0)]
        far = across(doc_embed, 2, 0, 1)
    docs, pools, place, at = pl.pallas_call(
        lambda *refs: pool_kernel((docs_dev, is_direct(columns), direct), blocks, *refs),
        out_shape=(
            shape(docs_dev, width, bf16),
            shape(4 * recs, width, bf16),
            shape(4 * recs, 128, jnp.int32),
            shape(8, 128, jnp.int32),
        ),
        in_specs=[pl.BlockSpec(memory_space=pltpu.HBM)] * 6,
        out_specs=(VMEM,) * 4,
        scratch_shapes=[
            pltpu.SMEM(frame_counts.shape, jnp.int32),
            pltpu.SMEM(doc_index.shape, jnp.int32),
            pltpu.VMEM(pool_query.shape, bf16),
            pltpu.VMEM(features.shape, bf16),
            pltpu.VMEM(w_proj.shape, bf16),
            pltpu.SemaphoreType.DMA((recs + 5,)),
        ],
        compiler_params=pltpu.CompilerParams(vmem_limit_bytes=12 * 2**20),
        name="pool",
    )(
        *[
            pltpu.with_memory_space_constraint(operand, pltpu.HBM)
            for operand in (frame_counts, doc_index, pool_query, features, w_proj, doc_embed)
        ]
    )
    other = to_other_core(pools)
    docs = [docs, *([far] if direct else [])]
    payload = [pools[: 2 * recs], other[: 2 * recs], pools[2 * recs : 3 * recs], other[2 * recs : 3 * recs]]
    payload = jnp.concatenate([*docs, *payload])
    parts = [payload]
    doc_rows = columns * (payload.shape[0] - 6 * recs)
    if is_direct(columns):
        parts += [across(payload, 0, steps) for steps in range(1, columns - 1)]
        parts.append(across(jnp.concatenate([*docs, pools]), 0, columns - 1, 1))
        parts.append(to_other_core(parts[-1][doc_rows // columns :]))
    else:
        parts = list(lax.all_gather(payload, "tm"))
    own, both = in_vmem(
        lambda *refs: meet_kernel(recs, heads, doc_rows // columns, is_direct(columns), *refs),
        (shape(doc_rows + 2 * recs, width, bf16), shape(4 * recs, width, bf16)),
        8,
        "meet",
    )(*parts)

    docs, near = own, []
    if direct:
        near = [across(own, 1, 0)]
        beyond = [across(both, steps, 0, 1) for steps in order]
    else:
        same_core = [[2 * n + core for n in range(layers)] for core in range(2)]
        docs = lax.all_gather(own[:doc_rows], "grp", axis_index_groups=same_core, tiled=True)
        docs = jnp.concatenate([docs, own[doc_rows:]])
    loss, grad = in_vmem(
        first_docs_kernel,
        (shape(4 * recs, 128), shape(4 * recs, width)),
        8 + docs.shape[0] // 128,
        "first_docs",
    )(place, both, docs)
    loss, grad, send = in_vmem(
        share_kernel,
        (shape(recs, 128), shape(recs, width), shape(4 * recs, width, bf16)),
        8,
        "share",
    )(place, both, loss, grad, *near)
    back = to_other_core(send)
    if direct:
        rows = (both, near[0][doc_rows:], *beyond)
    else:
        rows = (lax.all_gather(both[:recs], "grp", tiled=True),)
        at = doc_index[None, :] - (lax.axis_index("grp") * columns + lax.axis_index("tm")) * docs_dev
    loss, speech_grad, doc_grad = in_vmem(
        last_kernel,
        (shape(1, recs), shape(recs, width), shape(docs_dev, width)),
        8,
        "last",
    )(at, doc_embed, loss, grad, back, *rows)
    return (loss[0], speech_grad, doc_grad)


def solution(mesh):
    placed = (P("grp", "tm", None), P("grp"), P(), P(), P(("grp", "tm"), None), P())
    return jax.shard_map(
        body,
        mesh=mesh,
        in_specs=placed,
        out_specs=(P("grp"), P("grp", None), P(("grp", "tm"), None)),
        check_vma=False,
    )
```

```python
import math

import jax
import jax.numpy as jnp
from jax import lax
from jax.experimental import pallas as pl
from jax.experimental.pallas import tpu as pltpu
from jax.sharding import PartitionSpec as P

logit_scale = 10.0
logit_shift = -8.0
norm_eps = 1e-06
direct_limit = 8
bf16 = jnp.bfloat16
f32 = jnp.float32
BY_ROWS = (((1,), (1,)), ((), ()))
VMEM = pl.BlockSpec(memory_space=pltpu.VMEM)


def in_vmem(kernel, outs, limit_mib, name):
    def call(*operands):
        return pl.pallas_call(
            kernel,
            out_shape=outs,
            in_specs=[VMEM] * len(operands),
            out_specs=jax.tree.map(lambda _: VMEM, outs),
            compiler_params=pltpu.CompilerParams(vmem_limit_bytes=limit_mib * 2**20),
            name=name,
        )(*operands)

    return call


def two_terms(value):
    high = value.astype(bf16)
    return high, (value - high.astype(f32)).astype(bf16)


def pool_kernel(
    scheme,
    blocks,
    counts_hbm,
    index_hbm,
    query_hbm,
    features_hbm,
    proj_hbm,
    docs_hbm,
    docs_ref,
    out_ref,
    place_ref,
    at_ref,
    counts_ref,
    index_ref,
    query_ref,
    features_ref,
    proj_ref,
    sems,
):
    recs, frames, channels = features_ref.shape
    heads = query_ref.shape[0]
    width = proj_ref.shape[1]
    rows = recs * heads
    docs_dev, by_column, by_layer = scheme
    copies = [
        pltpu.make_async_copy(source, target, sems.at[n])
        for n, (source, target) in enumerate(
            [(counts_hbm, counts_ref), (index_hbm, index_ref), (query_hbm, query_ref)]
            + [(features_hbm.at[r], features_ref.at[r]) for r in range(recs)]
            + [(proj_hbm, proj_ref), (docs_hbm, docs_ref)]
        )
    ]
    for copy in copies:
        copy.start()
    copies[1].wait()
    group, column, tm = lax.axis_index("grp"), lax.axis_index("tm"), lax.axis_size("tm")
    layer, core = group // 2, group % 2
    row = lax.broadcasted_iota(jnp.int32, place_ref.shape, 0)
    spot = lax.broadcasted_iota(jnp.int32, place_ref.shape, 1)
    place = jnp.full(place_ref.shape, -1, jnp.int32)
    for r in range(2 * recs):
        target = index_ref[(group ^ (r // recs)) * recs + r % recs]
        of_group, rest = target // (tm * docs_dev), target % (tm * docs_dev)
        of_layer = of_group // 2
        at = (rest // docs_dev) ^ (column if by_column else 0)
        crossed = of_group + core
        if by_column:
            crossed = crossed + jnp.where(at == tm - 1, 1, 0)
        if by_layer:
            steps = of_layer ^ layer
            far = steps // 2
            at = (at * 2 + far) * docs_dev + rest % docs_dev
            chunk = steps % 2
            crossed = crossed + far
        else:
            at = (of_layer * tm + at) * docs_dev + rest % docs_dev
            chunk = 0
        mine = crossed % 2 == 0
        chunk = jnp.where(mine, chunk, -1)
        place = jnp.where((row == r) & (spot == chunk), at, place)
    place_ref[...] = place
    spot = lax.broadcasted_iota(jnp.int32, at_ref.shape, 1)
    ats = jnp.full(at_ref.shape, -1, jnp.int32)
    first = (group * tm + column) * docs_dev
    for n, block in enumerate(blocks):
        if block is not None:
            base = ((layer ^ block[0]) * 2 + (core ^ block[1])) * recs
            for r in range(recs):
                ats = jnp.where(spot == n * recs + r, index_ref[base + r] - first, ats)
    at_ref[...] = ats
    copies[0].wait()
    copies[2].wait()
    query = jnp.concatenate([query_ref[...].astype(f32), jnp.zeros((128 - heads, channels), f32)], 0).T.astype(bf16)
    start = lax.axis_index("tm") * frames
    spots = lax.broadcasted_iota(jnp.int32, (heads, frames), 1)
    scores, weights, peaks, totals, highs, lows = [], [], [], [], [], []
    for step in range(recs + 2):
        if step < recs:
            copies[3 + step].wait()
            scores.append(
                jnp.dot(features_ref[step], query, preferred_element_type=f32).T[:heads]
            )
        if 0 <= step - 1 < recs:
            r = step - 1
            valid = spots < counts_ref[r] - start
            masked = jnp.where(valid, scores[r] / math.sqrt(channels), -1e30)
            peak = jnp.max(masked, axis=1, keepdims=True).astype(bf16).astype(f32)
            weight = jnp.where(valid, jnp.exp(masked - peak), 0.0)
            peaks.append(peak)
            totals.append(jnp.sum(weight, axis=1, keepdims=True))
            weights.append(jnp.concatenate(two_terms(weight), 0))
        if 0 <= step - 2 < recs:
            r = step - 2
            both = jnp.dot(weights[r], features_ref[r], preferred_element_type=f32)
            high, low = two_terms(both[:heads] + both[heads:])
            highs.append(high)
            lows.append(low)
    peak, totals = jnp.concatenate(peaks, 0), jnp.concatenate(totals, 0)
    copies[3 + recs].wait()
    wide = jnp.dot(jnp.concatenate(highs + lows, 0), proj_ref[...], preferred_element_type=f32)
    wide = wide[:rows] + wide[rows:]
    own = lax.broadcasted_iota(jnp.int32, (rows, width), 1) // (width // heads)
    own = own == lax.broadcasted_iota(jnp.int32, (rows, width), 0) % heads
    lane = lax.broadcasted_iota(jnp.int32, (rows, 128), 1)
    lane = lane == lax.broadcasted_iota(jnp.int32, (rows, 128), 0) % heads

    def over_heads(value):
        return jnp.concatenate(
            [jnp.sum(value[r * heads : (r + 1) * heads], 0, keepdims=True) for r in range(recs)], 0
        )

    pooled = over_heads(jnp.where(own, wide, 0.0))
    pooled_high = pooled.astype(bf16).astype(f32)
    totals = over_heads(jnp.where(lane, totals, 0.0))
    totals_high = totals.astype(bf16).astype(f32)
    peaks = over_heads(jnp.where(lane, peak, 0.0))
    stats = [peaks, totals_high, totals - totals_high, jnp.zeros((recs, width - 384), f32)]
    copies[4 + recs].wait()
    out_ref[...] = jnp.concatenate(
        [pooled_high, pooled - pooled_high, jnp.concatenate(stats, 1), jnp.zeros((recs, width), f32)], 0
    ).astype(bf16)


def meet_kernel(recs, heads, doc_rows, apart, *refs):
    parts, (send_ref, both_ref) = list(refs[:-2]), refs[-2:]
    width = parts[0].shape[1]
    last = [parts.pop(), parts.pop()][::-1] if apart else []
    sums, peaks, totals = [], [], []
    for part in parts:
        pool = part[...].astype(f32)[doc_rows:]
        sums.append([pool[n : n + recs] + pool[n + recs : n + 2 * recs] for n in (0, 2 * recs)])
        peaks.append(pool[4 * recs :, :128])
        totals.append(pool[4 * recs :, 128:256] + pool[4 * recs :, 256:384])
    if apart:
        pools = [part[...].astype(f32)[part.shape[0] - 4 * recs :] for part in last[::-1]]
        sums.append([pool[:recs] + pool[recs : 2 * recs] for pool in pools])
        stats = jnp.concatenate([pool[2 * recs : 3 * recs] for pool in pools], 0)
        peaks.append(stats[:, :128])
        totals.append(stats[:, 128:256] + stats[:, 256:384])
        parts.append(last[0])
    sums = [jnp.concatenate(pair, 0) for pair in sums]
    top = peaks[0]
    for peak in peaks[1:]:
        top = jnp.maximum(top, peak)
    shares = [jnp.exp(peak - top) for peak in peaks]
    whole = shares[0] * totals[0]
    for share, total in zip(shares[1:], totals[1:]):
        whole = whole + share * total
    used = lax.broadcasted_iota(jnp.int32, whole.shape, 1) < heads
    inverse = jnp.where(used, 1.0 / jnp.where(used, whole, 1.0), 0.0)
    high, low = two_terms(jnp.concatenate([share * inverse for share in shares], 0))
    spread = lax.broadcasted_iota(jnp.int32, (16, width), 1) // (width // heads)
    spread = (spread == lax.broadcasted_iota(jnp.int32, (16, width), 0)).astype(f32).astype(bf16)
    scales = jnp.dot(jnp.concatenate([high, low], 0)[:, :16], spread, preferred_element_type=f32)
    scales = scales[: high.shape[0]] + scales[high.shape[0] :]
    pooled = jnp.zeros((2 * recs, width), f32)
    for n, part in enumerate(sums):
        pooled = pooled + part * scales[2 * n * recs : 2 * (n + 1) * recs]
    speech = pooled * lax.rsqrt(jnp.sum(pooled * pooled, axis=1, keepdims=True) + norm_eps)
    both_ref[...] = jnp.concatenate([speech, jnp.zeros((2 * recs, width), f32)], 0).astype(bf16)
    send_ref[...] = jnp.concatenate([part[:doc_rows, :] for part in parts] + [speech.astype(bf16)], 0)


def pair_terms(logits, positive):
    logits = logit_scale * logits + logit_shift
    signed = jnp.where(positive, -logits, logits)
    decay = jnp.exp(-jnp.abs(signed))
    losses = jnp.maximum(signed, 0.0) + jnp.log1p(decay)
    slopes = jnp.where(signed < 0.0, decay, 1.0) / (1.0 + decay)
    return losses, jnp.where(positive, -slopes, slopes).astype(bf16)


def speech_terms(place_ref, chunk, speech, docs):
    logits = lax.dot_general(speech, docs, BY_ROWS, preferred_element_type=f32)
    positive = lax.broadcasted_iota(jnp.int32, logits.shape, 1) == place_ref[:, chunk : chunk + 1]
    losses, grad_b = pair_terms(logits, positive)
    grad = logit_scale * jnp.dot(grad_b, docs, preferred_element_type=f32)
    return jnp.sum(losses, axis=1, keepdims=True), grad


def first_docs_kernel(place_ref, both_ref, docs_ref, loss_ref, grad_ref):
    recs = both_ref.shape[0] // 4
    loss, grad = speech_terms(place_ref, 0, both_ref[...], docs_ref[: docs_ref.shape[0] - 2 * recs, :])
    loss_ref[...] = jnp.broadcast_to(loss, loss_ref.shape)
    grad_ref[...] = grad


def share_kernel(place_ref, both_ref, loss_ref, grad_ref, *refs):
    blocks, (loss_out, grad_out, send_ref) = refs[:-3], refs[-3:]
    recs = both_ref.shape[0] // 4
    loss, grad = loss_ref[...], grad_ref[...]
    for block in blocks:
        doc_rows = block.shape[0] - 2 * recs
        more = speech_terms(place_ref, 1, both_ref[...], block[:doc_rows, :])
        loss, grad = loss + more[0], grad + more[1]
    loss_out[...] = loss[:recs]
    grad_out[...] = grad[:recs]
    loss, grad = loss[recs : 2 * recs], grad[recs : 2 * recs]
    grad_high = grad.astype(bf16).astype(f32)
    loss_high = loss.astype(bf16).astype(f32)
    loss_low = (loss - loss_high).astype(bf16).astype(f32)
    terms = [loss_high, loss_low, loss - loss_high - loss_low]
    terms.append(jnp.zeros((recs, grad.shape[1] - 384), f32))
    send_ref[...] = jnp.concatenate(
        [grad_high, grad - grad_high, jnp.concatenate(terms, 1)], 0
    ).astype(bf16)


def last_kernel(at_ref, docs_ref, loss_ref, grad_ref, back_ref, *refs):
    row_refs, (loss_out, speech_out, doc_out) = refs[:-3], refs[-3:]
    recs = speech_out.shape[0]
    back = back_ref[...].astype(f32)
    speech_out[...] = grad_ref[...] + back[:recs] + back[recs : 2 * recs]
    terms = back[2 * recs : 3 * recs]
    loss = loss_ref[...] + (terms[:, :128] + terms[:, 128:256] + terms[:, 256:384])
    diagonal = lax.broadcasted_iota(jnp.int32, (recs, 128), 0)
    diagonal = diagonal == lax.broadcasted_iota(jnp.int32, (recs, 128), 1)
    loss_out[...] = jnp.sum(jnp.where(diagonal, loss, 0.0), axis=0, keepdims=True)[:, :recs]
    if len(row_refs) == 1:
        rows = row_refs[0][...]
    else:
        both, near, *beyond = [ref[...].astype(f32) for ref in row_refs]
        beyond = [part[: 2 * recs] for part in beyond]
        rows = jnp.concatenate([both, near, *beyond], 0).astype(bf16)
    logits = lax.dot_general(docs_ref[...], rows, BY_ROWS, preferred_element_type=f32)
    positive = lax.broadcasted_iota(jnp.int32, logits.shape, 0) == at_ref[:1, : logits.shape[1]]
    _, grad_b = pair_terms(logits, positive)
    doc_out[...] = logit_scale * jnp.dot(grad_b, rows, preferred_element_type=f32)


def swap_pairs(count, stride, steps):
    return [(source, source ^ (steps * stride)) for source in range(count)]


def is_direct(extent):
    return extent <= direct_limit and extent & (extent - 1) == 0


def to_other_core(value):
    return lax.ppermute(value, "grp", swap_pairs(lax.axis_size("grp"), 1, 1))


def across(value, layer_steps, column_steps, core_steps=0):
    columns = lax.axis_size("tm")
    steps = (2 * layer_steps + core_steps) * columns + column_steps
    return lax.ppermute(value, ("grp", "tm"), swap_pairs(lax.axis_size("grp") * columns, 1, steps))


def body(features, frame_counts, pool_query, w_proj, doc_embed, doc_index):
    recs, frames, channels = features.shape
    heads, width = pool_query.shape[0], w_proj.shape[1]
    docs_dev = doc_embed.shape[0]
    groups, columns = lax.axis_size("grp"), lax.axis_size("tm")
    layers = groups // 2
    direct = layers == 4
    order = (2, 3) if direct else ()

    def shape(rows, lanes, kind=f32):
        return jax.ShapeDtypeStruct((rows, lanes), kind)

    blocks = []
    if direct:
        blocks = [(0, 0), (0, 1), None, None, (1, 0), (1, 1)]
        blocks += [(steps, flip) for steps in order for flip in (1, 0)]
        far = across(doc_embed, 2, 0, 1)
    docs, pools, place, at = pl.pallas_call(
        lambda *refs: pool_kernel((docs_dev, is_direct(columns), direct), blocks, *refs),
        out_shape=(
            shape(docs_dev, width, bf16),
            shape(4 * recs, width, bf16),
            shape(4 * recs, 128, jnp.int32),
            shape(8, 128, jnp.int32),
        ),
        in_specs=[pl.BlockSpec(memory_space=pltpu.HBM)] * 6,
        out_specs=(VMEM,) * 4,
        scratch_shapes=[
            pltpu.SMEM(frame_counts.shape, jnp.int32),
            pltpu.SMEM(doc_index.shape, jnp.int32),
            pltpu.VMEM(pool_query.shape, bf16),
            pltpu.VMEM(features.shape, bf16),
            pltpu.VMEM(w_proj.shape, bf16),
            pltpu.SemaphoreType.DMA((recs + 5,)),
        ],
        compiler_params=pltpu.CompilerParams(vmem_limit_bytes=12 * 2**20),
        name="pool",
    )(
        *[
            pltpu.with_memory_space_constraint(operand, pltpu.HBM)
            for operand in (frame_counts, doc_index, pool_query, features, w_proj, doc_embed)
        ]
    )
    other = to_other_core(pools)
    docs = [docs, *([far] if direct else [])]
    payload = [pools[: 2 * recs], other[: 2 * recs], pools[2 * recs : 3 * recs], other[2 * recs : 3 * recs]]
    payload = jnp.concatenate([*docs, *payload])
    parts = [payload]
    doc_rows = columns * (payload.shape[0] - 6 * recs)
    if is_direct(columns):
        parts += [across(payload, 0, steps) for steps in range(1, columns - 1)]
        parts.append(across(jnp.concatenate([*docs, pools]), 0, columns - 1, 1))
        parts.append(to_other_core(parts[-1][doc_rows // columns :]))
    else:
        parts = list(lax.all_gather(payload, "tm"))
    own, both = in_vmem(
        lambda *refs: meet_kernel(recs, heads, doc_rows // columns, is_direct(columns), *refs),
        (shape(doc_rows + 2 * recs, width, bf16), shape(4 * recs, width, bf16)),
        8,
        "meet",
    )(*parts)

    docs, near = own, []
    if direct:
        near = [across(own, 1, 0)]
        beyond = [across(both, steps, 0, 1) for steps in order]
    else:
        same_core = [[2 * n + core for n in range(layers)] for core in range(2)]
        docs = lax.all_gather(own[:doc_rows], "grp", axis_index_groups=same_core, tiled=True)
        docs = jnp.concatenate([docs, own[doc_rows:]])
    loss, grad = in_vmem(
        first_docs_kernel,
        (shape(4 * recs, 128), shape(4 * recs, width)),
        8 + docs.shape[0] // 128,
        "first_docs",
    )(place, both, docs)
    loss, grad, send = in_vmem(
        share_kernel,
        (shape(recs, 128), shape(recs, width), shape(3 * recs, width, bf16)),
        8,
        "share",
    )(place, both, loss, grad, *near)
    back = to_other_core(send)
    if direct:
        rows = (both, near[0][doc_rows:], *beyond)
    else:
        rows = (lax.all_gather(both[:recs], "grp", tiled=True),)
        at = doc_index[None, :] - (lax.axis_index("grp") * columns + lax.axis_index("tm")) * docs_dev
    loss, speech_grad, doc_grad = in_vmem(
        last_kernel,
        (shape(1, recs), shape(recs, width), shape(docs_dev, width)),
        8,
        "last",
    )(at, doc_embed, loss, grad, back, *rows)
    return (loss[0], speech_grad, doc_grad)


def solution(mesh):
    placed = (P("grp", "tm", None), P("grp"), P(), P(), P(("grp", "tm"), None), P())
    return jax.shard_map(
        body,
        mesh=mesh,
        in_specs=placed,
        out_specs=(P("grp"), P("grp", None), P(("grp", "tm"), None)),
        check_vma=False,
    )
```

```python
import math

import jax
import jax.numpy as jnp
from jax import lax
from jax.experimental import pallas as pl
from jax.experimental.pallas import tpu as pltpu
from jax.sharding import PartitionSpec as P

logit_scale = 10.0
logit_shift = -8.0
norm_eps = 1e-06
direct_limit = 8
bf16 = jnp.bfloat16
f32 = jnp.float32
BY_ROWS = (((1,), (1,)), ((), ()))
VMEM = pl.BlockSpec(memory_space=pltpu.VMEM)


def in_vmem(kernel, outs, limit_mib, name):
    def call(*operands):
        return pl.pallas_call(
            kernel,
            out_shape=outs,
            in_specs=[VMEM] * len(operands),
            out_specs=jax.tree.map(lambda _: VMEM, outs),
            compiler_params=pltpu.CompilerParams(vmem_limit_bytes=limit_mib * 2**20),
            name=name,
        )(*operands)

    return call


def two_terms(value):
    high = value.astype(bf16)
    return high, (value - high.astype(f32)).astype(bf16)


def pool_kernel(
    scheme,
    blocks,
    counts_hbm,
    index_hbm,
    query_hbm,
    features_hbm,
    proj_hbm,
    docs_hbm,
    docs_ref,
    out_ref,
    place_ref,
    at_ref,
    counts_ref,
    index_ref,
    query_ref,
    features_ref,
    proj_ref,
    sems,
):
    recs, frames, channels = features_ref.shape
    heads = query_ref.shape[0]
    width = proj_ref.shape[1]
    rows = recs * heads
    docs_dev, by_column, by_layer = scheme
    copies = [
        pltpu.make_async_copy(source, target, sems.at[n])
        for n, (source, target) in enumerate(
            [(counts_hbm, counts_ref), (index_hbm, index_ref), (query_hbm, query_ref)]
            + [(features_hbm.at[r], features_ref.at[r]) for r in range(recs)]
            + [(proj_hbm, proj_ref), (docs_hbm, docs_ref)]
        )
    ]
    for copy in copies:
        copy.start()
    copies[1].wait()
    group, column, tm = lax.axis_index("grp"), lax.axis_index("tm"), lax.axis_size("tm")
    layer, core = group // 2, group % 2
    row = lax.broadcasted_iota(jnp.int32, place_ref.shape, 0)
    spot = lax.broadcasted_iota(jnp.int32, place_ref.shape, 1)
    place = jnp.full(place_ref.shape, -1, jnp.int32)
    for r in range(2 * recs):
        target = index_ref[(group ^ (r // recs)) * recs + r % recs]
        of_group, rest = target // (tm * docs_dev), target % (tm * docs_dev)
        of_layer = of_group // 2
        at = (rest // docs_dev) ^ (column if by_column else 0)
        crossed = of_group + core
        if by_column:
            crossed = crossed + jnp.where(at == tm - 1, 1, 0)
        if by_layer:
            steps = of_layer ^ layer
            far = steps // 2
            at = (at * 2 + far) * docs_dev + rest % docs_dev
            chunk = steps % 2
            crossed = crossed + far
        else:
            at = (of_layer * tm + at) * docs_dev + rest % docs_dev
            chunk = 0
        mine = crossed % 2 == 0
        chunk = jnp.where(mine, chunk, -1)
        place = jnp.where((row == r) & (spot == chunk), at, place)
    place_ref[...] = place
    spot = lax.broadcasted_iota(jnp.int32, at_ref.shape, 1)
    ats = jnp.full(at_ref.shape, -1, jnp.int32)
    first = (group * tm + column) * docs_dev
    for n, block in enumerate(blocks):
        if block is not None:
            base = ((layer ^ block[0]) * 2 + (core ^ block[1])) * recs
            for r in range(recs):
                ats = jnp.where(spot == n * recs + r, index_ref[base + r] - first, ats)
    at_ref[...] = ats
    copies[0].wait()
    copies[2].wait()
    query = jnp.concatenate([query_ref[...].astype(f32), jnp.zeros((128 - heads, channels), f32)], 0).T.astype(bf16)
    start = lax.axis_index("tm") * frames
    spots = lax.broadcasted_iota(jnp.int32, (heads, frames), 1)
    scores, weights, peaks, totals, highs, lows = [], [], [], [], [], []
    for step in range(recs + 2):
        if step < recs:
            copies[3 + step].wait()
            scores.append(
                jnp.dot(features_ref[step], query, preferred_element_type=f32).T[:heads]
            )
        if 0 <= step - 1 < recs:
            r = step - 1
            valid = spots < counts_ref[r] - start
            masked = jnp.where(valid, scores[r] / math.sqrt(channels), -1e30)
            peak = jnp.max(masked, axis=1, keepdims=True).astype(bf16).astype(f32)
            weight = jnp.where(valid, jnp.exp(masked - peak), 0.0)
            peaks.append(peak)
            totals.append(jnp.sum(weight, axis=1, keepdims=True))
            weights.append(jnp.concatenate(two_terms(weight), 0))
        if 0 <= step - 2 < recs:
            r = step - 2
            both = jnp.dot(weights[r], features_ref[r], preferred_element_type=f32)
            high, low = two_terms(both[:heads] + both[heads:])
            highs.append(high)
            lows.append(low)
    peak, totals = jnp.concatenate(peaks, 0), jnp.concatenate(totals, 0)
    copies[3 + recs].wait()
    wide = jnp.dot(jnp.concatenate(highs + lows, 0), proj_ref[...], preferred_element_type=f32)
    wide = wide[:rows] + wide[rows:]
    own = lax.broadcasted_iota(jnp.int32, (rows, width), 1) // (width // heads)
    own = own == lax.broadcasted_iota(jnp.int32, (rows, width), 0) % heads
    lane = lax.broadcasted_iota(jnp.int32, (rows, 128), 1)
    lane = lane == lax.broadcasted_iota(jnp.int32, (rows, 128), 0) % heads

    def over_heads(value):
        return jnp.concatenate(
            [jnp.sum(value[r * heads : (r + 1) * heads], 0, keepdims=True) for r in range(recs)], 0
        )

    pooled = over_heads(jnp.where(own, wide, 0.0))
    pooled_high = pooled.astype(bf16).astype(f32)
    totals = over_heads(jnp.where(lane, totals, 0.0))
    totals_high = totals.astype(bf16).astype(f32)
    peaks = over_heads(jnp.where(lane, peak, 0.0))
    stats = [peaks, totals_high, totals - totals_high, jnp.zeros((recs, width - 384), f32)]
    copies[4 + recs].wait()
    out_ref[...] = jnp.concatenate(
        [pooled_high, pooled - pooled_high, jnp.concatenate(stats, 1), jnp.zeros((recs, width), f32)], 0
    ).astype(bf16)


def meet_kernel(recs, heads, doc_rows, apart, *refs):
    parts, (send_ref, both_ref) = list(refs[:-2]), refs[-2:]
    width = parts[0].shape[1]
    last = [parts.pop(), parts.pop()][::-1] if apart else []
    sums, peaks, totals = [], [], []
    for part in parts:
        pool = part[...].astype(f32)[doc_rows:]
        sums.append([pool[n : n + recs] + pool[n + recs : n + 2 * recs] for n in (0, 2 * recs)])
        peaks.append(pool[4 * recs :, :128])
        totals.append(pool[4 * recs :, 128:256] + pool[4 * recs :, 256:384])
    if apart:
        pools = [part[...].astype(f32)[part.shape[0] - 4 * recs :] for part in last[::-1]]
        sums.append([pool[:recs] + pool[recs : 2 * recs] for pool in pools])
        stats = jnp.concatenate([pool[2 * recs : 3 * recs] for pool in pools], 0)
        peaks.append(stats[:, :128])
        totals.append(stats[:, 128:256] + stats[:, 256:384])
        parts.append(last[0])
    sums = [jnp.concatenate(pair, 0) for pair in sums]
    top = peaks[0]
    for peak in peaks[1:]:
        top = jnp.maximum(top, peak)
    shares = [jnp.exp(peak - top) for peak in peaks]
    whole = shares[0] * totals[0]
    for share, total in zip(shares[1:], totals[1:]):
        whole = whole + share * total
    used = lax.broadcasted_iota(jnp.int32, whole.shape, 1) < heads
    inverse = jnp.where(used, 1.0 / jnp.where(used, whole, 1.0), 0.0)
    high, low = two_terms(jnp.concatenate([share * inverse for share in shares], 0))
    spread = lax.broadcasted_iota(jnp.int32, (16, width), 1) // (width // heads)
    spread = (spread == lax.broadcasted_iota(jnp.int32, (16, width), 0)).astype(f32).astype(bf16)
    scales = jnp.dot(jnp.concatenate([high, low], 0)[:, :16], spread, preferred_element_type=f32)
    scales = scales[: high.shape[0]] + scales[high.shape[0] :]
    pooled = jnp.zeros((2 * recs, width), f32)
    for n, part in enumerate(sums):
        pooled = pooled + part * scales[2 * n * recs : 2 * (n + 1) * recs]
    speech = pooled * lax.rsqrt(jnp.sum(pooled * pooled, axis=1, keepdims=True) + norm_eps)
    both_ref[...] = jnp.concatenate([speech, jnp.zeros((2 * recs, width), f32)], 0).astype(bf16)
    send_ref[...] = jnp.concatenate([part[:doc_rows, :] for part in parts] + [speech.astype(bf16)], 0)


def pair_terms(logits, positive):
    logits = logit_scale * logits + logit_shift
    signed = jnp.where(positive, -logits, logits)
    losses = jnp.maximum(signed, 0.0) + jnp.log1p(jnp.exp(-jnp.abs(signed)))
    slopes = jax.nn.sigmoid(signed)
    return losses, jnp.where(positive, -slopes, slopes).astype(bf16)


def speech_terms(place_ref, chunk, speech, docs):
    logits = lax.dot_general(speech, docs, BY_ROWS, preferred_element_type=f32)
    positive = lax.broadcasted_iota(jnp.int32, logits.shape, 1) == place_ref[:, chunk : chunk + 1]
    losses, grad_b = pair_terms(logits, positive)
    grad = logit_scale * jnp.dot(grad_b, docs, preferred_element_type=f32)
    return jnp.sum(losses, axis=1, keepdims=True), grad


def first_docs_kernel(place_ref, both_ref, docs_ref, loss_ref, grad_ref):
    recs = both_ref.shape[0] // 4
    loss, grad = speech_terms(place_ref, 0, both_ref[...], docs_ref[: docs_ref.shape[0] - 2 * recs, :])
    loss_ref[...] = jnp.broadcast_to(loss, loss_ref.shape)
    grad_ref[...] = grad


def share_kernel(place_ref, both_ref, loss_ref, grad_ref, *refs):
    blocks, (loss_out, grad_out, send_ref) = refs[:-3], refs[-3:]
    recs = both_ref.shape[0] // 4
    loss, grad = loss_ref[...], grad_ref[...]
    for block in blocks:
        doc_rows = block.shape[0] - 2 * recs
        more = speech_terms(place_ref, 1, both_ref[...], block[:doc_rows, :])
        loss, grad = loss + more[0], grad + more[1]
    loss_out[...] = loss[:recs]
    grad_out[...] = grad[:recs]
    loss, grad = loss[recs : 2 * recs], grad[recs : 2 * recs]
    grad_high = grad.astype(bf16).astype(f32)
    loss_high = loss.astype(bf16).astype(f32)
    loss_low = (loss - loss_high).astype(bf16).astype(f32)
    terms = [loss_high, loss_low, loss - loss_high - loss_low]
    terms.append(jnp.zeros((recs, grad.shape[1] - 384), f32))
    send_ref[...] = jnp.concatenate(
        [grad_high, grad - grad_high, jnp.concatenate(terms, 1), jnp.zeros_like(grad)], 0
    ).astype(bf16)


def last_kernel(at_ref, docs_ref, loss_ref, grad_ref, back_ref, *refs):
    row_refs, (loss_out, speech_out, doc_out) = refs[:-3], refs[-3:]
    recs = speech_out.shape[0]
    back = back_ref[...].astype(f32)
    speech_out[...] = grad_ref[...] + back[:recs] + back[recs : 2 * recs]
    terms = back[2 * recs : 3 * recs]
    loss = loss_ref[...] + (terms[:, :128] + terms[:, 128:256] + terms[:, 256:384])
    diagonal = lax.broadcasted_iota(jnp.int32, (recs, 128), 0)
    diagonal = diagonal == lax.broadcasted_iota(jnp.int32, (recs, 128), 1)
    loss_out[...] = jnp.sum(jnp.where(diagonal, loss, 0.0), axis=0, keepdims=True)[:, :recs]
    if len(row_refs) == 1:
        rows = row_refs[0][...]
    else:
        both, near, *beyond = [ref[...].astype(f32) for ref in row_refs]
        beyond = [part[: 2 * recs] for part in beyond]
        rows = jnp.concatenate([both, near, *beyond], 0).astype(bf16)
    logits = lax.dot_general(docs_ref[...], rows, BY_ROWS, preferred_element_type=f32)
    positive = lax.broadcasted_iota(jnp.int32, logits.shape, 0) == at_ref[:1, : logits.shape[1]]
    _, grad_b = pair_terms(logits, positive)
    doc_out[...] = logit_scale * jnp.dot(grad_b, rows, preferred_element_type=f32)


def swap_pairs(count, stride, steps):
    return [(source, source ^ (steps * stride)) for source in range(count)]


def is_direct(extent):
    return extent <= direct_limit and extent & (extent - 1) == 0


def to_other_core(value):
    return lax.ppermute(value, "grp", swap_pairs(lax.axis_size("grp"), 1, 1))


def across(value, layer_steps, column_steps, core_steps=0):
    columns = lax.axis_size("tm")
    steps = (2 * layer_steps + core_steps) * columns + column_steps
    return lax.ppermute(value, ("grp", "tm"), swap_pairs(lax.axis_size("grp") * columns, 1, steps))


def body(features, frame_counts, pool_query, w_proj, doc_embed, doc_index):
    recs, frames, channels = features.shape
    heads, width = pool_query.shape[0], w_proj.shape[1]
    docs_dev = doc_embed.shape[0]
    groups, columns = lax.axis_size("grp"), lax.axis_size("tm")
    layers = groups // 2
    direct = layers == 4
    order = (2, 3) if direct else ()

    def shape(rows, lanes, kind=f32):
        return jax.ShapeDtypeStruct((rows, lanes), kind)

    blocks = []
    if direct:
        blocks = [(0, 0), (0, 1), None, None, (1, 0), (1, 1)]
        blocks += [(steps, flip) for steps in order for flip in (steps % 2, 1 - steps % 2)]
        far = across(doc_embed, 2, 0, 1)
    docs, pools, place, at = pl.pallas_call(
        lambda *refs: pool_kernel((docs_dev, is_direct(columns), direct), blocks, *refs),
        out_shape=(
            shape(docs_dev, width, bf16),
            shape(4 * recs, width, bf16),
            shape(4 * recs, 128, jnp.int32),
            shape(8, 128, jnp.int32),
        ),
        in_specs=[pl.BlockSpec(memory_space=pltpu.HBM)] * 6,
        out_specs=(VMEM,) * 4,
        scratch_shapes=[
            pltpu.SMEM(frame_counts.shape, jnp.int32),
            pltpu.SMEM(doc_index.shape, jnp.int32),
            pltpu.VMEM(pool_query.shape, bf16),
            pltpu.VMEM(features.shape, bf16),
            pltpu.VMEM(w_proj.shape, bf16),
            pltpu.SemaphoreType.DMA((recs + 5,)),
        ],
        compiler_params=pltpu.CompilerParams(vmem_limit_bytes=12 * 2**20),
        name="pool",
    )(
        *[
            pltpu.with_memory_space_constraint(operand, pltpu.HBM)
            for operand in (frame_counts, doc_index, pool_query, features, w_proj, doc_embed)
        ]
    )
    other = to_other_core(pools)
    docs = [docs, *([far] if direct else [])]
    payload = [pools[: 2 * recs], other[: 2 * recs], pools[2 * recs : 3 * recs], other[2 * recs : 3 * recs]]
    payload = jnp.concatenate([*docs, *payload])
    parts = [payload]
    doc_rows = columns * (payload.shape[0] - 6 * recs)
    if is_direct(columns):
        parts += [across(payload, 0, steps) for steps in range(1, columns - 1)]
        parts.append(across(jnp.concatenate([*docs, pools]), 0, columns - 1, 1))
        parts.append(to_other_core(parts[-1][doc_rows // columns :]))
    else:
        parts = list(lax.all_gather(payload, "tm"))
    own, both = in_vmem(
        lambda *refs: meet_kernel(recs, heads, doc_rows // columns, is_direct(columns), *refs),
        (shape(doc_rows + 2 * recs, width, bf16), shape(4 * recs, width, bf16)),
        8,
        "meet",
    )(*parts)

    docs, near = own, []
    if direct:
        near = [across(own, 1, 0)]
        beyond = [across(both, steps, 0, steps % 2) for steps in order]
    else:
        same_core = [[2 * n + core for n in range(layers)] for core in range(2)]
        docs = lax.all_gather(own[:doc_rows], "grp", axis_index_groups=same_core, tiled=True)
        docs = jnp.concatenate([docs, own[doc_rows:]])
    loss, grad = in_vmem(
        first_docs_kernel,
        (shape(4 * recs, 128), shape(4 * recs, width)),
        8 + docs.shape[0] // 128,
        "first_docs",
    )(place, both, docs)
    loss, grad, send = in_vmem(
        share_kernel,
        (shape(recs, 128), shape(recs, width), shape(4 * recs, width, bf16)),
        8,
        "share",
    )(place, both, loss, grad, *near)
    back = to_other_core(send)
    if direct:
        rows = (both, near[0][doc_rows:], *beyond)
    else:
        rows = (lax.all_gather(both[:recs], "grp", tiled=True),)
        at = doc_index[None, :] - (lax.axis_index("grp") * columns + lax.axis_index("tm")) * docs_dev
    loss, speech_grad, doc_grad = in_vmem(
        last_kernel,
        (shape(1, recs), shape(recs, width), shape(docs_dev, width)),
        8,
        "last",
    )(at, doc_embed, loss, grad, back, *rows)
    return (loss[0], speech_grad, doc_grad)


def solution(mesh):
    placed = (P("grp", "tm", None), P("grp"), P(), P(), P(("grp", "tm"), None), P())
    return jax.shard_map(
        body,
        mesh=mesh,
        in_specs=placed,
        out_specs=(P("grp"), P("grp", None), P(("grp", "tm"), None)),
        check_vma=False,
    )
```
